512 devices in a mesh: depth: 8 (over z_hi, core), lat: 64 (over x, z_lo, y).
Axes of the slice: x: 4, y: 4, z: 16 (z_hi: 4, z_lo: 4; z = z_hi * 4 + z_lo), core: 2. Of those that a mesh axis runs over, the one named last changes fastest.
Arguments:
- fields: float32 [6, 384, 64, 512], P(None, 'lat', 'depth'), may hold values from -3 to 3
- material: int32 [384, 64, 512], P('lat', 'depth'), may hold values from 0 to 3
- source_mask: int32 [384, 64, 512], P('lat', 'depth'), may hold values 0 or 1
- eps_table: float32 [4], replicated, may hold values from 1 to 6
- kerr_table: float32 [4], replicated, may hold values from 0.3 to 3
Outputs:
- fields_out: float32 [6, 384, 64, 512], P(None, 'lat', 'depth')
- image: float32 [384, 8, 512], P('lat', None, 'depth')
The draws below stay inside these ranges and needn't reach their ends.
Inputs may be any that keep to these rules, and one draw needn't show every extreme that they name: material indexes the tables.
All inputs are finite; a program needn't handle non-finite values. No bound on the sum of `source_mask` on one device may be relied on, other than what follows from the above.
Results may differ from the reference program's by a relative error of at most 0.0003.
Values sent between devices are 32-bit elements; how exact they have to be, the bound alone decides.
A program may use at most 64 MiB of HBM per device.

```python
import math
import jax
import jax.numpy as jnp
from jax import lax

NY = 512
STEPS = 16
MATERIALS = 4
NX = 384
NZ = 64


def set_ends(array, own_key, smallest, high):
    dims = array.shape
    place = [jax.random.randint(jax.random.fold_in(own_key, axis), (), 0, dims[axis]) for axis in range(len(dims))]
    array = array.at[tuple(place)].set(smallest)
    longest = dims.index(max(dims))
    place[longest] = (place[longest] + 1) % dims[longest]
    return array.at[tuple(place)].set(high)


def steps_of(own_key, dims, pieces, low, top_value):
    def one(axis_at, parts):
        draws = jax.random.uniform(jax.random.fold_in(jax.random.fold_in(own_key, 6), axis_at), (parts,), jnp.float32, low / len(pieces), top_value / len(pieces))
        return jnp.repeat(jnp.exp(draws), dims[axis_at] // parts).reshape((-1,) + (1,) * (len(dims) - axis_at - 1))

    factor_of = one(*pieces[0])
    for cut in pieces[1:]:
        factor_of = factor_of * one(*cut)
    return factor_of


def centred(own_key, dims, deviation, limit, split=(), kind=jnp.bfloat16):
    entries = deviation * jax.random.normal(own_key, dims, jnp.float32)
    if split:
        entries = entries * steps_of(own_key, dims, split, -0.22, 0.18)
    return jnp.clip(entries, -limit, limit).astype(kind)


def setup_inputs(seed: int = 0) -> dict:
    arg_keys = jax.random.split(jax.random.key(seed), 6)
    return {
        "fields": centred(arg_keys[0], (6, NX, NZ, NY), 0.5, 3.0, ((1, 64), (2, 8)), jnp.float32),
        "material": set_ends(jax.random.randint(arg_keys[1], (NX, NZ, NY), 0, MATERIALS), jax.random.fold_in(arg_keys[1], 1), 0, MATERIALS - 1).astype(jnp.int32),
        "source_mask": set_ends((jax.random.randint(arg_keys[2], (NX, NZ, NY), 0, 8) < 1).astype(jnp.int32), jax.random.fold_in(arg_keys[2], 1), 0, 1),
        "eps_table": jnp.clip(jax.random.uniform(arg_keys[3], (MATERIALS,), jnp.float32, 1.0, 6.0), 1.0, 6.0),
        "kerr_table": jnp.clip(jnp.exp(jax.random.uniform(arg_keys[4], (MATERIALS,), jnp.float32, math.log(0.3), math.log(3.0))), 0.3, 3.0),
    }


COURANT = 0.55
OMEGAS = (0.9, 1.3)
SOURCE_AMP = 1.0
QUARTERS = (3, 5)
HIGHEST = lax.Precision.HIGHEST

def forward_diff(field, along):
    length = field.shape[along]
    ahead = lax.slice_in_dim(field, 1, length, axis=along)
    ahead = jnp.concatenate([ahead, jnp.zeros_like(lax.slice_in_dim(field, 0, 1, axis=along))], axis=along)
    return ahead - field

def backward_diff(field, along):
    length = field.shape[along]
    behind = lax.slice_in_dim(field, 0, length - 1, axis=along)
    behind = jnp.concatenate([jnp.zeros_like(lax.slice_in_dim(field, 0, 1, axis=along)), behind], axis=along)
    return field - behind

def drive(moment):
    middle = moment + 0.5
    return SOURCE_AMP * (jnp.sin(OMEGAS[0] * middle) + jnp.sin(OMEGAS[1] * middle))

def yee_step(fields, permittivity, kerr_coef, source_flag, inside, pulse):
    elec_x, elec_y, elec_z = (fields[0], fields[1], fields[2])
    magn_x, magn_y, magn_z = (fields[3], fields[4], fields[5])
    magn_x = (magn_x - COURANT * (forward_diff(elec_z, 2) - forward_diff(elec_y, 1))) * inside
    magn_y = (magn_y - COURANT * (forward_diff(elec_x, 1) - forward_diff(elec_z, 0))) * inside
    magn_z = (magn_z - COURANT * (forward_diff(elec_y, 0) - forward_diff(elec_x, 2))) * inside
    energy = elec_x * elec_x + elec_y * elec_y + elec_z * elec_z
    factor = COURANT / (permittivity + kerr_coef * energy)
    new_x = (elec_x + factor * (backward_diff(magn_z, 2) - backward_diff(magn_y, 1)) + source_flag * pulse) * inside
    new_y = (elec_y + factor * (backward_diff(magn_x, 1) - backward_diff(magn_z, 0))) * inside
    new_z = (elec_z + factor * (backward_diff(magn_y, 0) - backward_diff(magn_x, 2))) * inside
    return jnp.stack([new_x, new_y, new_z, magn_x, magn_y, magn_z])

def lookup(material, table):
    result = jnp.zeros(material.shape, jnp.float32)
    for level in range(table.shape[0]):
        result = jnp.where(material == level, table[level], result)
    return result

def accumulate(spectrum, plane, moment):
    later = moment + 1.0
    trig = jnp.stack([jnp.stack([jnp.cos(omega * later), -jnp.sin(omega * later)]) for omega in OMEGAS])
    return spectrum + trig[:, None, :, None, None] * plane[None, :, None, :, :]

def chirp(row_index, col_index, length):
    gap = row_index[:, None] - col_index[None, :]
    squared = gap * gap
    reals, imags = ([], [])
    for quarter in QUARTERS:
        wrapped = quarter * squared % (8 * length)
        phase = wrapped.astype(jnp.float32) * (math.pi / (4.0 * length))
        reals.append(jnp.cos(phase) / math.sqrt(length))
        imags.append(jnp.sin(phase) / math.sqrt(length))
    return (jnp.stack(reals), jnp.stack(imags))

def column_transform(real, imag, y_real, y_imag):
    v_real = jnp.einsum('fcxy,fyk->fcxk', real, y_real, precision=HIGHEST) - jnp.einsum('fcxy,fyk->fcxk', imag, y_imag, precision=HIGHEST)
    v_imag = jnp.einsum('fcxy,fyk->fcxk', real, y_imag, precision=HIGHEST) + jnp.einsum('fcxy,fyk->fcxk', imag, y_real, precision=HIGHEST)
    return (v_real, v_imag)

def row_transform(x_real, x_imag, v_real, v_imag):
    w_real = jnp.einsum('fix,fcxk->ifck', x_real, v_real, precision=HIGHEST) - jnp.einsum('fix,fcxk->ifck', x_imag, v_imag, precision=HIGHEST)
    w_imag = jnp.einsum('fix,fcxk->ifck', x_real, v_imag, precision=HIGHEST) + jnp.einsum('fix,fcxk->ifck', x_imag, v_real, precision=HIGHEST)
    return jnp.stack([w_real, w_imag], axis=3)

def reference(fields, material, source_mask, eps_table, kerr_table):
    permittivity = lookup(material, eps_table)
    kerr_coef = lookup(material, kerr_table)
    source_flag = source_mask.astype(jnp.float32)
    spectrum = jnp.zeros((2, 2, 2, NX, NY), jnp.float32)
    for step in range(STEPS):
        moment = jnp.float32(step)
        fields = yee_step(fields, permittivity, kerr_coef, source_flag, 1.0, drive(moment))
        spectrum = accumulate(spectrum, fields[0:2, :, NZ - 1, :], moment)
    y_index = jnp.arange(NY, dtype=jnp.int32)
    x_index = jnp.arange(NX, dtype=jnp.int32)
    y_real, y_imag = chirp(y_index, y_index, NY)
    x_real, x_imag = chirp(x_index, x_index, NX)
    v_real, v_imag = column_transform(spectrum[:, :, 0], spectrum[:, :, 1], y_real, y_imag)
    image = row_transform(x_real, x_imag, v_real, v_imag)
    return (fields, image.reshape(NX, 8, NY))
```

```python
import functools
import math

import jax
import jax.numpy as jnp
import numpy as np
from jax import lax
from jax.experimental import pallas as pl
from jax.experimental.pallas import tpu as pltpu
from jax.sharding import PartitionSpec as P

STEPS = 16
COURANT = 0.55
OMEGAS = (0.9, 1.3)
QUARTERS = (3, 5)
HIGHEST = lax.Precision.HIGHEST
MESH = pl.DeviceIdType.MESH


def pulses():
    middle = np.arange(STEPS) + 0.5
    return np.asarray(np.sin(OMEGAS[0] * middle) + np.sin(OMEGAS[1] * middle), np.float32)


def turns():
    later = np.arange(STEPS) + 1.0
    parts = []
    for omega in OMEGAS:
        parts += [np.cos(omega * later), -np.sin(omega * later)]
    return np.asarray(np.stack(parts, axis=1), np.float32)


def chirp(length):
    gap = np.arange(length)[:, None] - np.arange(length)[None, :]
    reals, imags = [], []
    for quarter in QUARTERS:
        phase = (quarter * gap * gap % (8 * length)) * (math.pi / (4.0 * length))
        reals.append(np.cos(phase) / math.sqrt(length))
        imags.append(np.sin(phase) / math.sqrt(length))
    return np.asarray(np.stack(reals), np.float32), np.asarray(np.stack(imags), np.float32)


def step_kernel(
    count_z, count_x,
    fields_ref, material_ref, mask_ref, eps_ref, kerr_ref, pulse_ref, turn_ref,
    state, spec,
    eps_v, kerr_v, src_v, fac_v,
    rows_e, rows_h, rows_top, corner_s,
    in_xe, in_xh, in_ze, in_zh, in_c,
    send_sem, recv_sem,
):
    wide = state.shape[1]
    span = state.shape[3]
    last = wide - 1
    pos_z = lax.axis_index("depth")
    pos_x = lax.axis_index("lat")
    has_lx, has_hx = pos_x > 0, pos_x < count_x - 1
    has_lz, has_hz = pos_z > 0, pos_z < count_z - 1
    has_a = has_lz & has_hx
    has_b = has_hz & has_lx
    to_lx, to_hx = (pos_z, pos_x - 1), (pos_z, pos_x + 1)
    to_lz, to_hz = (pos_z - 1, pos_x), (pos_z + 1, pos_x)
    to_a, to_b = (pos_z - 1, pos_x + 1), (pos_z + 1, pos_x - 1)
    neighbours = (
        (has_lx, to_lx), (has_hx, to_hx), (has_lz, to_lz), (has_hz, to_hz), (has_a, to_a), (has_b, to_b)
    )

    in_xe[...] = jnp.zeros_like(in_xe)
    in_xh[...] = jnp.zeros_like(in_xh)
    in_ze[...] = jnp.zeros_like(in_ze)
    in_zh[...] = jnp.zeros_like(in_zh)
    in_c[...] = jnp.zeros_like(in_c)

    barrier = pltpu.get_barrier_semaphore()
    for has, target in neighbours:
        @pl.when(has)
        def _():
            pl.semaphore_signal(barrier, inc=1, device_id=target, device_id_type=MESH)

    material = material_ref[...]
    eps, kerr = jnp.zeros(material.shape, jnp.float32), jnp.zeros(material.shape, jnp.float32)
    for level in range(eps_ref.shape[0]):
        eps = jnp.where(material == level, eps_ref[level], eps)
        kerr = jnp.where(material == level, kerr_ref[level], kerr)
    eps_v[...] = eps
    kerr_v[...] = kerr
    src_v[...] = mask_ref[...].astype(jnp.float32)
    state[...] = fields_ref[...]
    spec[...] = jnp.zeros_like(spec)

    pl.semaphore_wait(barrier, sum(jnp.where(has, 1, 0) for has, _ in neighbours))

    row = lax.broadcasted_iota(jnp.int32, (8, span), 0)
    col = lax.broadcasted_iota(jnp.int32, (8, span), 1)
    top_row, first_row = row == 7, row == 0
    top_col, first_col = col == span - 1, col == 0
    s = jnp.float32(COURANT)
    keep_lx = jnp.where(has_lx, 1.0, 0.0).astype(jnp.float32)
    keep_lz = jnp.where(has_lz, 1.0, 0.0).astype(jnp.float32)

    def next_y(f):
        return jnp.where(top_col, 0.0, pltpu.roll(f, span - 1, 1))

    def prev_y(f):
        return jnp.where(first_col, 0.0, pltpu.roll(f, 1, 1))

    def next_z(f):
        return jnp.where(top_row, 0.0, pltpu.roll(f, 7, 0))

    def wide_row(r):
        return jnp.broadcast_to(r, (8, span))

    def one_step(n, carry):
        slot = lax.rem(n, 2)

        def copy(index, source, target, there, sem):
            return pltpu.make_async_remote_copy(
                src_ref=source, dst_ref=there, send_sem=send_sem.at[index],
                recv_sem=recv_sem.at[slot, sem], device_id=target, device_id_type=MESH,
            )

        for x in range(wide):
            rows_e[0, x : x + 1, :] = state[0, x, 0:1, :]
            rows_e[1, x : x + 1, :] = state[1, x, 0:1, :]
        corner_s[0:1, :] = state[2, 0, 7:8, :]
        out_lx = copy(0, state.at[1:3, 0], to_lx, in_xe.at[slot], 0)
        out_lz = copy(1, rows_e, to_lz, in_ze.at[slot], 1)
        out_a = copy(2, rows_e.at[0, last : last + 1], to_a, in_c.at[slot, 0], 2)
        out_b = copy(3, corner_s, to_b, in_c.at[slot, 1], 3)
        for has, item in ((has_a, out_a), (has_b, out_b), (has_lx, out_lx), (has_lz, out_lz)):
            @pl.when(has)
            def _():
                item.start()

        for x in [last] + list(range(last)):
            ex, ey, ez = state[0, x], state[1, x], state[2, x]
            if x < last:
                ahead_y, ahead_z = state[1, x + 1], state[2, x + 1]
            else:
                ahead_y, ahead_z = jnp.zeros_like(ey), jnp.zeros_like(ez)
            hx = state[3, x] - s * ((next_y(ez) - ez) - (next_z(ey) - ey))
            hy = state[4, x] - s * ((next_z(ex) - ex) - (ahead_z - ez))
            hz = state[5, x] - s * ((ahead_y - ey) - (next_y(ex) - ex))
            state[3, x] = hx
            state[4, x] = hy
            state[5, x] = hz
            rows_h[0, x : x + 1, :] = hx[7:8, :]
            rows_h[1, x : x + 1, :] = hy[7:8, :]
        out_hx = copy(4, state.at[4:6, last], to_hx, in_xh.at[slot], 4)
        out_hz = copy(5, rows_h, to_hz, in_zh.at[slot], 5)
        for has, item in ((has_hz, out_hz), (has_hx, out_hx)):
            @pl.when(has)
            def _():
                item.start()

        for x in range(wide):
            ex, ey, ez = state[0, x], state[1, x], state[2, x]
            fac_v[x] = s / (eps_v[x] + kerr_v[x] * (ex * ex + ey * ey + ez * ez))

        for has, sem, there in (
            (has_hx, 0, in_xe), (has_lx, 4, in_xh), (has_hz, 1, in_ze), (has_lz, 5, in_zh),
        ):
            @pl.when(has)
            def _():
                pltpu.make_async_remote_copy(
                    src_ref=there.at[slot], dst_ref=there.at[slot], send_sem=send_sem.at[sem],
                    recv_sem=recv_sem.at[slot, sem], device_id=to_lx, device_id_type=MESH,
                ).wait_recv()
        for has, sem, place in ((has_b, 2, 0), (has_a, 3, 1)):
            @pl.when(has)
            def _():
                pltpu.make_async_remote_copy(
                    src_ref=in_c.at[slot, place], dst_ref=in_c.at[slot, place], send_sem=send_sem.at[sem],
                    recv_sem=recv_sem.at[slot, sem], device_id=to_lx, device_id_type=MESH,
                ).wait_recv()
        for has, item in (
            (has_lx, out_lx), (has_lz, out_lz), (has_a, out_a), (has_b, out_b), (has_hx, out_hx), (has_hz, out_hz)
        ):
            @pl.when(has)
            def _():
                item.wait_send()

        ex, ey, ez = state[0, 0], state[1, 0], state[2, 0]
        corner_x = jnp.where(top_row, wide_row(in_c[slot, 0]), 0.0)
        before_y = keep_lx * (in_xh[slot, 0] + s * ez - s * corner_x)
        before_z = keep_lx * (in_xh[slot, 1] - s * ey)
        pulse = pulse_ref[n]
        for x in range(wide):
            ex, ey, ez = state[0, x], state[1, x], state[2, x]
            above_x = wide_row(in_ze[slot, 0, x : x + 1, :])
            above_y = wide_row(in_ze[slot, 1, x : x + 1, :])
            hx = state[3, x] + jnp.where(top_row, s * above_y, 0.0)
            hy = state[4, x] - jnp.where(top_row, s * above_x, 0.0)
            hz = state[5, x]
            below_x = wide_row(in_zh[slot, 0, x : x + 1, :]) + s * ey
            below_y = wide_row(in_zh[slot, 1, x : x + 1, :]) - s * ex
            if x == last:
                hy = hy + s * in_xe[slot, 1]
                hz = hz - s * in_xe[slot, 0]
                below_y = below_y + s * wide_row(in_c[slot, 1])
            down_x = jnp.where(first_row, keep_lz * below_x, pltpu.roll(hx, 1, 0))
            down_y = jnp.where(first_row, keep_lz * below_y, pltpu.roll(hy, 1, 0))
            fac = fac_v[x]
            state[0, x] = ex + fac * ((hz - prev_y(hz)) - (hy - down_y)) + src_v[x] * pulse
            state[1, x] = ey + fac * ((hx - down_x) - (hz - before_z))
            state[2, x] = ez + fac * ((hy - before_y) - (hx - prev_y(hx)))
            state[3, x] = hx
            state[4, x] = hy
            state[5, x] = hz
            before_y, before_z = hy, hz

        @pl.when(pos_z == count_z - 1)
        def _():
            for x in range(wide):
                rows_top[0, x : x + 1, :] = state[0, x, 7:8, :]
                rows_top[1, x : x + 1, :] = state[1, x, 7:8, :]
            for f in range(2):
                for part in range(2):
                    weight = turn_ref[n, 2 * f + part]
                    for c in range(2):
                        spec[4 * f + 2 * c + part] += weight * rows_top[c]

        return carry

    lax.fori_loop(0, STEPS, one_step, 0)


def march(count_z, count_x, fields, material, mask, eps_table, kerr_table):
    _, wide, deep, span = fields.shape
    vmem = pl.BlockSpec(memory_space=pltpu.VMEM)
    smem = pl.BlockSpec(memory_space=pltpu.SMEM)
    f32 = jnp.float32
    return pl.pallas_call(
        functools.partial(step_kernel, count_z, count_x),
        out_shape=(
            jax.ShapeDtypeStruct(fields.shape, f32),
            jax.ShapeDtypeStruct((8, wide, span), f32),
        ),
        in_specs=[vmem, vmem, vmem, smem, smem, smem, smem],
        out_specs=(vmem, vmem),
        scratch_shapes=[
            pltpu.VMEM((wide, deep, span), f32),
            pltpu.VMEM((wide, deep, span), f32),
            pltpu.VMEM((wide, deep, span), f32),
            pltpu.VMEM((wide, deep, span), f32),
            pltpu.VMEM((2, wide, span), f32),
            pltpu.VMEM((2, wide, span), f32),
            pltpu.VMEM((2, wide, span), f32),
            pltpu.VMEM((1, span), f32),
            pltpu.VMEM((2, 2, deep, span), f32),
            pltpu.VMEM((2, 2, deep, span), f32),
            pltpu.VMEM((2, 2, wide, span), f32),
            pltpu.VMEM((2, 2, wide, span), f32),
            pltpu.VMEM((2, 2, 1, span), f32),
            pltpu.SemaphoreType.DMA((6,)),
            pltpu.SemaphoreType.DMA((2, 6)),
        ],
        compiler_params=pltpu.CompilerParams(
            collective_id=1, has_side_effects=True, vmem_limit_bytes=32 * 1024 * 1024
        ),
        name="march",
    )(fields, material, mask, eps_table, kerr_table, jnp.asarray(pulses()), jnp.asarray(turns()))


def local(fields, material, source_mask, eps_table, kerr_table):
    _, wide, deep, span = fields.shape
    count_x, count_z = lax.axis_size("lat"), lax.axis_size("depth")
    state, spec = march(count_z, count_x, fields, material, source_mask, eps_table, kerr_table)
    spec = spec.reshape(2, 2, 2, wide, span)
    y_real, y_imag = (jnp.asarray(part) for part in chirp(span))
    both = jnp.concatenate([y_real, y_imag], axis=2)
    prod = jnp.einsum("fcpxy,fyk->fcpxk", spec, both, precision=HIGHEST)
    v_real = prod[:, :, 0, :, :span] - prod[:, :, 1, :, span:]
    v_imag = prod[:, :, 0, :, span:] + prod[:, :, 1, :, :span]
    v = jnp.stack([v_real, v_imag])
    cols = span // count_z
    v = v.reshape(8 * wide, count_z, cols).transpose(1, 0, 2)
    v = lax.all_to_all(v, "depth", 0, 0)[count_z - 1]
    per = cols // count_x
    v = v.reshape(2, 2, 2, wide, count_x, per).transpose(4, 0, 1, 2, 3, 5)
    v = lax.all_to_all(v, "lat", 0, 0)
    v = v.transpose(2, 0, 4, 1, 3, 5).reshape(2, count_x * wide, 2 * 2 * per)
    x_real, x_imag = (jnp.asarray(part) for part in chirp(count_x * wide))
    both = jnp.concatenate([x_real, x_imag], axis=1)
    w = jnp.einsum("fix,fxn->fin", both, v, precision=HIGHEST)
    total = count_x * wide
    w = w.reshape(2, 2, total, 2, 2, per)
    w_real = w[:, 0, :, 0] - w[:, 1, :, 1]
    w_imag = w[:, 0, :, 1] + w[:, 1, :, 0]
    w = jnp.stack([w_real, w_imag], axis=3)
    w = w.transpose(1, 0, 2, 3, 4).reshape(count_x, wide, 8, per)
    w = lax.all_to_all(w, "lat", 0, 0)
    image = w.transpose(1, 2, 0, 3).reshape(wide, 8, cols)
    return state, image


def solution(mesh):
    placed = (P(None, "lat", "depth", None), P("lat", "depth", None), P("lat", "depth", None), P(), P())
    return jax.shard_map(
        local, mesh=mesh, in_specs=placed,
        out_specs=(P(None, "lat", "depth", None), P("lat", None, "depth")), check_vma=False,
    )
```

```python
import functools
import math

import jax
import jax.numpy as jnp
import numpy as np
from jax import lax
from jax.experimental import pallas as pl
from jax.experimental.pallas import tpu as pltpu
from jax.sharding import PartitionSpec as P

STEPS = 16
COURANT = 0.55
OMEGAS = (0.9, 1.3)
QUARTERS = (3, 5)
HIGHEST = lax.Precision.HIGHEST
MESH = pl.DeviceIdType.MESH


def pulses():
    middle = np.arange(STEPS) + 0.5
    return np.asarray(np.sin(OMEGAS[0] * middle) + np.sin(OMEGAS[1] * middle), np.float32)


def turns():
    later = np.arange(STEPS) + 1.0
    parts = []
    for omega in OMEGAS:
        parts += [np.cos(omega * later), -np.sin(omega * later)]
    return np.asarray(np.stack(parts, axis=1), np.float32)


def chirp(length):
    gap = np.arange(length)[:, None] - np.arange(length)[None, :]
    reals, imags = [], []
    for quarter in QUARTERS:
        phase = (quarter * gap * gap % (8 * length)) * (math.pi / (4.0 * length))
        reals.append(np.cos(phase) / math.sqrt(length))
        imags.append(np.sin(phase) / math.sqrt(length))
    return np.asarray(np.stack(reals), np.float32), np.asarray(np.stack(imags), np.float32)


def step_kernel(
    count_z, count_x,
    fields_hbm, material_hbm, mask_hbm, eps_hbm, kerr_hbm,
    state, spec,
    material_ref, mask_ref, eps_ref, kerr_ref, pulse_ref, turn_ref, load_sem,
    eps_v, kerr_v, src_v, fac_v,
    rows_e, rows_h, rows_top, corner_s, mix,
    in_xe, in_xr, in_xh, in_ze, in_zh, in_c,
    send_sem, recv_sem, corner_send, corner_recv,
):
    wide = state.shape[1]
    span = state.shape[3]
    last = wide - 1
    pos_z = lax.axis_index("depth")
    pos_x = lax.axis_index("lat")
    has_lx, has_hx = pos_x > 0, pos_x < count_x - 1
    has_lz, has_hz = pos_z > 0, pos_z < count_z - 1
    has_a = has_lz & has_hx
    has_b = has_hz & has_lx
    to_lx, to_hx = (pos_z, pos_x - 1), (pos_z, pos_x + 1)
    to_lz, to_hz = (pos_z - 1, pos_x), (pos_z + 1, pos_x)
    to_a, to_b = (pos_z - 1, pos_x + 1), (pos_z + 1, pos_x - 1)
    neighbours = (
        (has_lx, to_lx), (has_hx, to_hx), (has_lz, to_lz), (has_hz, to_hz), (has_a, to_a), (has_b, to_b)
    )

    loads = [
        pltpu.make_async_copy(source, there, load_sem.at[i])
        for i, (source, there) in enumerate((
            (material_hbm, material_ref), (mask_hbm, mask_ref), (eps_hbm, eps_ref), (kerr_hbm, kerr_ref),
            (fields_hbm, state),
        ))
    ]
    for item in loads:
        item.start()
    in_xe[...] = jnp.zeros_like(in_xe)
    in_xh[...] = jnp.zeros_like(in_xh)
    in_ze[...] = jnp.zeros_like(in_ze)
    in_zh[...] = jnp.zeros_like(in_zh)
    in_xr[...] = jnp.zeros_like(in_xr)
    in_c[...] = jnp.zeros_like(in_c)
    mix[...] = jnp.zeros_like(mix)

    barrier = pltpu.get_barrier_semaphore()
    for has, target in neighbours:
        @pl.when(has)
        def _():
            pl.semaphore_signal(barrier, inc=1, device_id=target, device_id_type=MESH)

    for n in range(STEPS):
        pulse_ref[n] = jnp.float32(pulses()[n])
        for i in range(4):
            turn_ref[4 * n + i] = jnp.float32(turns()[n, i])
    for item in loads:
        item.wait()
    material = material_ref[...]
    eps, kerr = jnp.zeros(material.shape, jnp.float32), jnp.zeros(material.shape, jnp.float32)
    for level in range(eps_ref.shape[0]):
        eps = jnp.where(material == level, eps_ref[level], eps)
        kerr = jnp.where(material == level, kerr_ref[level], kerr)
    eps_v[...] = eps
    kerr_v[...] = kerr
    src_v[...] = mask_ref[...].astype(jnp.float32)
    spec[...] = jnp.zeros_like(spec)

    pl.semaphore_wait(barrier, sum(jnp.where(has, 1, 0) for has, _ in neighbours))

    row = lax.broadcasted_iota(jnp.int32, (8, span), 0)
    col = lax.broadcasted_iota(jnp.int32, (8, span), 1)
    top_row, first_row = row == 7, row == 0
    top_col, first_col = col == span - 1, col == 0
    s = jnp.float32(COURANT)
    keep_lx = jnp.where(has_lx, 1.0, 0.0).astype(jnp.float32)
    keep_lz = jnp.where(has_lz, 1.0, 0.0).astype(jnp.float32)

    def next_y(f):
        return jnp.where(top_col, 0.0, pltpu.roll(f, span - 1, 1))

    def prev_y(f):
        return jnp.where(first_col, 0.0, pltpu.roll(f, 1, 1))

    def next_z(f):
        return jnp.where(top_row, 0.0, pltpu.roll(f, 7, 0))

    def wide_row(r):
        return jnp.broadcast_to(r, (8, span))

    def prev_row(r):
        return jnp.where(first_col[0:1], 0.0, pltpu.roll(r, 1, 1))

    def corner(when, place):
        return pltpu.make_async_remote_copy(
            src_ref=corner_s.at[lax.rem(when, 2), place], dst_ref=in_c.at[lax.rem(when, 4), place],
            send_sem=corner_send.at[lax.rem(when, 2), place], recv_sem=corner_recv.at[lax.rem(when, 4), place],
            device_id=(to_a, to_b)[place], device_id_type=MESH,
        )

    corner_s[...] = jnp.zeros_like(corner_s)
    corner_s[0, 0, 0:1, :] = state[0, last, 0:1, :]
    corner_s[0, 1, 0:1, :] = state[2, 0, 7:8, :]
    for place, has in ((0, has_a), (1, has_b)):
        @pl.when(has)
        def _():
            corner(0, place).start()

    def one_step(n, carry):
        slot = lax.rem(n, 2)

        def copy(index, source, target, there, sem):
            return pltpu.make_async_remote_copy(
                src_ref=source, dst_ref=there, send_sem=send_sem.at[index],
                recv_sem=recv_sem.at[slot, sem], device_id=target, device_id_type=MESH,
            )

        for x in range(wide):
            rows_e[0, x : x + 1, :] = state[0, x, 0:1, :]
            rows_e[1, x : x + 1, :] = state[1, x, 0:1, :]
        rows_e[0, wide : wide + 1, :] = state[2, 0, 0:1, :]
        rows_e[1, wide : wide + 1, :] = state[2, 0, 0:1, :]
        out_lx = copy(0, state.at[1:3, 0], to_lx, in_xe.at[slot], 0)
        out_lz = copy(1, rows_e, to_lz, in_ze.at[slot], 1)
        out_rx = copy(2, rows_e.at[0, 0:1], to_lx, in_xr.at[slot], 2)
        for has, item in ((has_lx, out_lx), (has_lz, out_lz), (has_lx, out_rx)):
            @pl.when(has)
            def _():
                item.start()

        for x in [last] + list(range(last)):
            ex, ey, ez = state[0, x], state[1, x], state[2, x]
            if x < last:
                ahead_y, ahead_z = state[1, x + 1], state[2, x + 1]
            else:
                ahead_y, ahead_z = jnp.zeros_like(ey), jnp.zeros_like(ez)
            hx = state[3, x] - s * ((next_y(ez) - ez) - (next_z(ey) - ey))
            hy = state[4, x] - s * ((next_z(ex) - ex) - (ahead_z - ez))
            hz = state[5, x] - s * ((ahead_y - ey) - (next_y(ex) - ex))
            state[3, x] = hx
            state[4, x] = hy
            state[5, x] = hz
            rows_h[0, x : x + 1, :] = hx[7:8, :]
            rows_h[1, x : x + 1, :] = hy[7:8, :]
        out_hx = copy(3, state.at[4:6, last], to_hx, in_xh.at[slot], 3)
        out_hz = copy(4, rows_h, to_hz, in_zh.at[slot], 4)
        for has, item in ((has_hz, out_hz), (has_hx, out_hx)):
            @pl.when(has)
            def _():
                item.start()

        for x in range(wide):
            ex, ey, ez = state[0, x], state[1, x], state[2, x]
            fac_v[x] = s / (eps_v[x] + kerr_v[x] * (ex * ex + ey * ey + ez * ez))

        pulse = pulse_ref[n]
        ahead = n + 1
        side = lax.rem(ahead, 2)
        corner_s[side, 0, 0:1, :] = (
            state[0, last, 0:1, :]
            + fac_v[last, 0:1, :] * (state[5, last, 0:1, :] - prev_row(state[5, last, 0:1, :]) - state[4, last, 0:1, :])
            + src_v[last, 0:1, :] * pulse
        )
        corner_s[side, 0, 1:2, :] = fac_v[last, 0:1, :]
        corner_s[side, 1, 0:1, :] = state[2, 0, 7:8, :] + fac_v[0, 7:8, :] * (
            state[4, 0, 7:8, :] - (state[3, 0, 7:8, :] - prev_row(state[3, 0, 7:8, :]))
        )
        corner_s[side, 1, 1:2, :] = fac_v[0, 7:8, :]
        for place, has in ((0, has_a), (1, has_b)):
            @pl.when(has & (ahead < STEPS))
            def _():
                corner(ahead, place).start()

        for has, index, there in (
            (has_hx, 0, in_xe), (has_lx, 3, in_xh), (has_hz, 1, in_ze), (has_lz, 4, in_zh), (has_hx, 2, in_xr),
        ):
            @pl.when(has)
            def _():
                copy(index, there.at[slot], to_lx, there.at[slot], index).wait_recv()
        for has, item in (
            (has_lx, out_lx), (has_lz, out_lz), (has_lx, out_rx), (has_hx, out_hx), (has_hz, out_hz)
        ):
            @pl.when(has)
            def _():
                item.wait_send()
        for place, has_to, has_from in ((0, has_a, has_b), (1, has_b, has_a)):
            @pl.when(has_from)
            def _():
                corner(n, place).wait_recv()

            @pl.when(has_to)
            def _():
                corner(n, place).wait_send()
        here = lax.rem(n, 4)
        corner_ex = in_c[here, 0, 0:1, :] + in_c[here, 0, 1:2, :] * mix[0:1, :]
        corner_ez = in_c[here, 1, 0:1, :] + in_c[here, 1, 1:2, :] * mix[1:2, :]

        ex, ey, ez = state[0, 0], state[1, 0], state[2, 0]
        corner_x = jnp.where(top_row, wide_row(corner_ex), 0.0)
        before_y = keep_lx * (in_xh[slot, 0] + s * ez - s * corner_x)
        before_z = keep_lx * (in_xh[slot, 1] - s * ey)
        face = in_ze[slot, 1, 0:1, :]
        mix[0:1, :] = before_y[7:8, :] - s * (face - prev_row(face)) - s * in_ze[slot, 0, wide : wide + 1, :]
        for x in range(wide):
            ex, ey, ez = state[0, x], state[1, x], state[2, x]
            above_x = wide_row(in_ze[slot, 0, x : x + 1, :])
            above_y = wide_row(in_ze[slot, 1, x : x + 1, :])
            hx = state[3, x] + jnp.where(top_row, s * above_y, 0.0)
            hy = state[4, x] - jnp.where(top_row, s * above_x, 0.0)
            hz = state[5, x]
            below_x = wide_row(in_zh[slot, 0, x : x + 1, :]) + s * ey
            below_y = wide_row(in_zh[slot, 1, x : x + 1, :]) - s * ex
            if x == last:
                hy = hy + s * in_xe[slot, 1]
                hz = hz - s * in_xe[slot, 0]
                below_y = below_y + s * wide_row(corner_ez)
                face = in_xe[slot, 0, 0:1, :]
                mix[1:2, :] = -below_y[0:1, :] - s * in_xr[slot] - s * (face - prev_row(face))
            down_x = jnp.where(first_row, keep_lz * below_x, pltpu.roll(hx, 1, 0))
            down_y = jnp.where(first_row, keep_lz * below_y, pltpu.roll(hy, 1, 0))
            fac = fac_v[x]
            state[0, x] = ex + fac * ((hz - prev_y(hz)) - (hy - down_y)) + src_v[x] * pulse
            state[1, x] = ey + fac * ((hx - down_x) - (hz - before_z))
            state[2, x] = ez + fac * ((hy - before_y) - (hx - prev_y(hx)))
            state[3, x] = hx
            state[4, x] = hy
            state[5, x] = hz
            before_y, before_z = hy, hz

        @pl.when(pos_z == count_z - 1)
        def _():
            for x in range(wide):
                rows_top[0, x : x + 1, :] = state[0, x, 7:8, :]
                rows_top[1, x : x + 1, :] = state[1, x, 7:8, :]
            for f in range(2):
                for part in range(2):
                    weight = turn_ref[4 * n + 2 * f + part]
                    for c in range(2):
                        spec[4 * f + 2 * c + part] += weight * rows_top[c]

        return carry

    lax.fori_loop(0, STEPS, one_step, 0)


def march(count_z, count_x, fields, material, mask, eps_table, kerr_table):
    _, wide, deep, span = fields.shape
    vmem = pl.BlockSpec(memory_space=pltpu.VMEM)
    f32 = jnp.float32
    return pl.pallas_call(
        functools.partial(step_kernel, count_z, count_x),
        out_shape=(
            jax.ShapeDtypeStruct(fields.shape, f32),
            jax.ShapeDtypeStruct((8, wide, span), f32),
        ),
        in_specs=[pl.BlockSpec(memory_space=pl.ANY)] * 5,
        out_specs=(vmem, vmem),
        scratch_shapes=[
            pltpu.VMEM((wide, deep, span), jnp.int32),
            pltpu.VMEM((wide, deep, span), jnp.int32),
            pltpu.SMEM(eps_table.shape, f32),
            pltpu.SMEM(kerr_table.shape, f32),
            pltpu.SMEM((STEPS,), f32),
            pltpu.SMEM((4 * STEPS,), f32),
            pltpu.SemaphoreType.DMA((5,)),
            pltpu.VMEM((wide, deep, span), f32),
            pltpu.VMEM((wide, deep, span), f32),
            pltpu.VMEM((wide, deep, span), f32),
            pltpu.VMEM((wide, deep, span), f32),
            pltpu.VMEM((2, wide + 1, span), f32),
            pltpu.VMEM((2, wide, span), f32),
            pltpu.VMEM((2, wide, span), f32),
            pltpu.VMEM((2, 2, 2, span), f32),
            pltpu.VMEM((2, span), f32),
            pltpu.VMEM((2, 2, deep, span), f32),
            pltpu.VMEM((2, 1, span), f32),
            pltpu.VMEM((2, 2, deep, span), f32),
            pltpu.VMEM((2, 2, wide + 1, span), f32),
            pltpu.VMEM((2, 2, wide, span), f32),
            pltpu.VMEM((4, 2, 2, span), f32),
            pltpu.SemaphoreType.DMA((5,)),
            pltpu.SemaphoreType.DMA((2, 5)),
            pltpu.SemaphoreType.DMA((2, 2)),
            pltpu.SemaphoreType.DMA((4, 2)),
        ],
        compiler_params=pltpu.CompilerParams(
            collective_id=1, has_side_effects=True, vmem_limit_bytes=60 * 1024 * 1024
        ),
        name="march",
    )(fields, material, mask, eps_table, kerr_table)


def local(fields, material, source_mask, eps_table, kerr_table):
    _, wide, deep, span = fields.shape
    count_x, count_z = lax.axis_size("lat"), lax.axis_size("depth")
    state, spec = march(count_z, count_x, fields, material, source_mask, eps_table, kerr_table)
    spec = spec.reshape(2, 2, 2, wide, span)
    y_real, y_imag = (jnp.asarray(part) for part in chirp(span))
    both = jnp.concatenate([y_real, y_imag], axis=2)
    prod = jnp.einsum("fcpxy,fyk->fcpxk", spec, both, precision=HIGHEST)
    v_real = prod[:, :, 0, :, :span] - prod[:, :, 1, :, span:]
    v_imag = prod[:, :, 0, :, span:] + prod[:, :, 1, :, :span]
    v = jnp.stack([v_real, v_imag])
    cols = span // count_z
    v = v.reshape(8 * wide, count_z, cols).transpose(1, 0, 2)
    v = lax.all_to_all(v, "depth", 0, 0)[count_z - 1]
    per = cols // count_x
    v = v.reshape(2, 2, 2, wide, count_x, per).transpose(4, 0, 1, 2, 3, 5)
    v = lax.all_to_all(v, "lat", 0, 0)
    v = v.transpose(2, 0, 4, 1, 3, 5).reshape(2, count_x * wide, 2 * 2 * per)
    x_real, x_imag = (jnp.asarray(part) for part in chirp(count_x * wide))
    both = jnp.concatenate([x_real, x_imag], axis=1)
    w = jnp.einsum("fix,fxn->fin", both, v, precision=HIGHEST)
    total = count_x * wide
    w = w.reshape(2, 2, total, 2, 2, per)
    w_real = w[:, 0, :, 0] - w[:, 1, :, 1]
    w_imag = w[:, 0, :, 1] + w[:, 1, :, 0]
    w = jnp.stack([w_real, w_imag], axis=3)
    w = w.transpose(1, 0, 2, 3, 4).reshape(count_x, wide, 8, per)
    w = lax.all_to_all(w, "lat", 0, 0)
    image = w.transpose(1, 2, 0, 3).reshape(wide, 8, cols)
    return state, image


def solution(mesh):
    placed = (P(None, "lat", "depth", None), P("lat", "depth", None), P("lat", "depth", None), P(), P())
    return jax.shard_map(
        local, mesh=mesh, in_specs=placed,
        out_specs=(P(None, "lat", "depth", None), P("lat", None, "depth")), check_vma=False,
    )
```

```python
import functools
import math

import jax
import jax.numpy as jnp
import numpy as np
from jax import lax
from jax.experimental import pallas as pl
from jax.experimental.pallas import tpu as pltpu
from jax.sharding import PartitionSpec as P

STEPS = 16
COURANT = 0.55
OMEGAS = (0.9, 1.3)
QUARTERS = (3, 5)
MESH = pl.DeviceIdType.MESH


def pulses():
    middle = np.arange(STEPS) + 0.5
    return np.asarray(np.sin(OMEGAS[0] * middle) + np.sin(OMEGAS[1] * middle), np.float32)


def turns():
    later = np.arange(STEPS) + 1.0
    parts = []
    for omega in OMEGAS:
        parts += [np.cos(omega * later), -np.sin(omega * later)]
    return np.asarray(np.stack(parts, axis=1), np.float32)


def split(table):
    high = table.astype(jnp.bfloat16)
    return high, (table - high.astype(np.float32)).astype(jnp.bfloat16)


def chirp(length, run):
    gap = np.arange(length)[:, None] - np.arange(length)[None, :]
    padded = -(-run // 8) * 8
    tables = []
    for quarter in QUARTERS:
        phase = (quarter * gap * gap % (8 * length)) * (math.pi / (4.0 * length))
        table = np.stack([np.cos(phase), np.sin(phase)], axis=1) / math.sqrt(length)
        table = table.reshape(length // run, run, 2, length // run, run)
        table = np.pad(table, ((0, 0), (0, padded - run), (0, 0), (0, 0), (0, padded - run)))
        tables.append(table.reshape(length // run * padded, 2 * (length // run) * padded))
    return split(np.asarray(np.stack(tables), np.float32))


def step_kernel(
    count_z, count_x,
    fields_hbm, material_hbm, mask_hbm, eps_hbm, kerr_hbm, col_high_hbm, col_low_hbm, row_high_hbm, row_low_hbm,
    state, image,
    spec, col_high, col_low, row_high, row_low, table_sem, planes, out_a, in_a, out_b, in_b, tail_send, tail_recv,
    material_ref, mask_ref, eps_ref, kerr_ref, pulse_ref, turn_ref, load_sem,
    eps_v, kerr_v, src_v, fac_v,
    rows_e, rows_h, rows_top, corner_s, mix,
    in_xe, in_xr, in_xh, in_ze, in_zh, in_c,
    send_sem, recv_sem, corner_send, corner_recv,
):
    wide = state.shape[1]
    span = state.shape[3]
    last = wide - 1
    pos_z = lax.axis_index("depth")
    pos_x = lax.axis_index("lat")
    has_lx, has_hx = pos_x > 0, pos_x < count_x - 1
    has_lz, has_hz = pos_z > 0, pos_z < count_z - 1
    has_a = has_lz & has_hx
    has_b = has_hz & has_lx
    to_lx, to_hx = (pos_z, pos_x - 1), (pos_z, pos_x + 1)
    to_lz, to_hz = (pos_z - 1, pos_x), (pos_z + 1, pos_x)
    to_a, to_b = (pos_z - 1, pos_x + 1), (pos_z + 1, pos_x - 1)
    neighbours = (
        (has_lx, to_lx), (has_hx, to_hx), (has_lz, to_lz), (has_hz, to_hz), (has_a, to_a), (has_b, to_b)
    )

    loads = [
        pltpu.make_async_copy(source, there, load_sem.at[i])
        for i, (source, there) in enumerate((
            (material_hbm, material_ref), (mask_hbm, mask_ref), (eps_hbm, eps_ref), (kerr_hbm, kerr_ref),
            (fields_hbm, state),
        ))
    ]
    for item in loads:
        item.start()
    in_xe[...] = jnp.zeros_like(in_xe)
    in_xh[...] = jnp.zeros_like(in_xh)
    in_ze[...] = jnp.zeros_like(in_ze)
    in_zh[...] = jnp.zeros_like(in_zh)
    in_xr[...] = jnp.zeros_like(in_xr)
    in_c[...] = jnp.zeros_like(in_c)
    mix[...] = jnp.zeros_like(mix)

    barrier = pltpu.get_barrier_semaphore()
    for has, target in neighbours:
        @pl.when(has)
        def _():
            pl.semaphore_signal(barrier, inc=1, device_id=target, device_id_type=MESH)

    exit_z = count_z - 1
    at_exit = pos_z == exit_z
    group = count_x // count_z
    for j in range(group):
        sender = pos_z * group + j
        @pl.when(jnp.logical_not(at_exit & (sender == pos_x)))
        def _():
            pl.semaphore_signal(barrier, inc=1, device_id=(exit_z, sender), device_id_type=MESH)

    tables = [
        pltpu.make_async_copy(source, there, table_sem.at[i])
        for i, (source, there) in enumerate((
            (col_high_hbm, col_high), (col_low_hbm, col_low), (row_high_hbm, row_high), (row_low_hbm, row_low)
        ))
    ]

    @pl.when(at_exit)
    def _():
        def greet(i, carry):
            pl.semaphore_signal(
                barrier, inc=1, device_id=(exit_z, lax.rem(pos_x + i, count_x)), device_id_type=MESH
            )
            return carry

        lax.fori_loop(1, count_x, greet, 0)
        for item in tables:
            item.start()

    for n in range(STEPS):
        pulse_ref[n] = jnp.float32(pulses()[n])
        for i in range(4):
            turn_ref[4 * n + i] = jnp.float32(turns()[n, i])
    for item in loads:
        item.wait()
    material = material_ref[...]
    eps, kerr = jnp.zeros(material.shape, jnp.float32), jnp.zeros(material.shape, jnp.float32)
    for level in range(eps_ref.shape[0]):
        eps = jnp.where(material == level, eps_ref[level], eps)
        kerr = jnp.where(material == level, kerr_ref[level], kerr)
    eps_v[...] = eps
    kerr_v[...] = kerr
    src_v[...] = mask_ref[...].astype(jnp.float32)
    spec[...] = jnp.zeros_like(spec)
    rows_top[...] = jnp.zeros_like(rows_top)

    target_z = pos_x // group
    greeted = sum(jnp.where(has, 1, 0) for has, _ in neighbours)
    greeted += jnp.where(at_exit, 2 * count_x - 1 - jnp.where(target_z == exit_z, 1, 0), 0)
    pl.semaphore_wait(barrier, greeted)

    row = lax.broadcasted_iota(jnp.int32, (8, span), 0)
    col = lax.broadcasted_iota(jnp.int32, (8, span), 1)
    top_row, first_row = row == 7, row == 0
    top_col, first_col = col == span - 1, col == 0
    s = jnp.float32(COURANT)
    keep_lx = jnp.where(has_lx, 1.0, 0.0).astype(jnp.float32)
    keep_lz = jnp.where(has_lz, 1.0, 0.0).astype(jnp.float32)

    def next_y(f):
        return jnp.where(top_col, 0.0, pltpu.roll(f, span - 1, 1))

    def prev_y(f):
        return jnp.where(first_col, 0.0, pltpu.roll(f, 1, 1))

    def next_z(f):
        return jnp.where(top_row, 0.0, pltpu.roll(f, 7, 0))

    def wide_row(r):
        return jnp.broadcast_to(r, (8, span))

    def prev_row(r):
        return jnp.where(first_col[0:1], 0.0, pltpu.roll(r, 1, 1))

    def corner(when, place):
        return pltpu.make_async_remote_copy(
            src_ref=corner_s.at[lax.rem(when, 2), place], dst_ref=in_c.at[lax.rem(when, 4), place],
            send_sem=corner_send.at[lax.rem(when, 2), place], recv_sem=corner_recv.at[lax.rem(when, 4), place],
            device_id=(to_a, to_b)[place], device_id_type=MESH,
        )

    corner_s[...] = jnp.zeros_like(corner_s)
    corner_s[0, 0, 0:1, :] = state[0, last, 0:1, :]
    corner_s[0, 1, 0:1, :] = state[2, 0, 7:8, :]
    for place, has in ((0, has_a), (1, has_b)):
        @pl.when(has)
        def _():
            corner(0, place).start()

    def one_step(n, carry):
        slot = lax.rem(n, 2)

        def copy(index, source, target, there, sem):
            return pltpu.make_async_remote_copy(
                src_ref=source, dst_ref=there, send_sem=send_sem.at[index],
                recv_sem=recv_sem.at[slot, sem], device_id=target, device_id_type=MESH,
            )

        for x in range(wide):
            rows_e[0, x : x + 1, :] = state[0, x, 0:1, :]
            rows_e[1, x : x + 1, :] = state[1, x, 0:1, :]
        rows_e[0, wide : wide + 1, :] = state[2, 0, 0:1, :]
        rows_e[1, wide : wide + 1, :] = state[2, 0, 0:1, :]
        out_lx = copy(0, state.at[1:3, 0], to_lx, in_xe.at[slot], 0)
        out_lz = copy(1, rows_e, to_lz, in_ze.at[slot], 1)
        out_rx = copy(2, rows_e.at[0, 0:1], to_lx, in_xr.at[slot], 2)
        for has, item in ((has_lx, out_lx), (has_lz, out_lz), (has_lx, out_rx)):
            @pl.when(has)
            def _():
                item.start()

        for x in [last] + list(range(last)):
            ex, ey, ez = state[0, x], state[1, x], state[2, x]
            if x < last:
                ahead_y, ahead_z = state[1, x + 1], state[2, x + 1]
            else:
                ahead_y, ahead_z = jnp.zeros_like(ey), jnp.zeros_like(ez)
            hx = state[3, x] - s * ((next_y(ez) - ez) - (next_z(ey) - ey))
            hy = state[4, x] - s * ((next_z(ex) - ex) - (ahead_z - ez))
            hz = state[5, x] - s * ((ahead_y - ey) - (next_y(ex) - ex))
            state[3, x] = hx
            state[4, x] = hy
            state[5, x] = hz
            rows_h[0, x : x + 1, :] = hx[7:8, :]
            rows_h[1, x : x + 1, :] = hy[7:8, :]
        out_hx = copy(3, state.at[4:6, last], to_hx, in_xh.at[slot], 3)
        out_hz = copy(4, rows_h, to_hz, in_zh.at[slot], 4)
        for has, item in ((has_hz, out_hz), (has_hx, out_hx)):
            @pl.when(has)
            def _():
                item.start()

        for x in range(wide):
            ex, ey, ez = state[0, x], state[1, x], state[2, x]
            fac_v[x] = s / (eps_v[x] + kerr_v[x] * (ex * ex + ey * ey + ez * ez))

        pulse = pulse_ref[n]
        ahead = n + 1
        side = lax.rem(ahead, 2)
        corner_s[side, 0, 0:1, :] = (
            state[0, last, 0:1, :]
            + fac_v[last, 0:1, :] * (state[5, last, 0:1, :] - prev_row(state[5, last, 0:1, :]) - state[4, last, 0:1, :])
            + src_v[last, 0:1, :] * pulse
        )
        corner_s[side, 0, 1:2, :] = fac_v[last, 0:1, :]
        corner_s[side, 1, 0:1, :] = state[2, 0, 7:8, :] + fac_v[0, 7:8, :] * (
            state[4, 0, 7:8, :] - (state[3, 0, 7:8, :] - prev_row(state[3, 0, 7:8, :]))
        )
        corner_s[side, 1, 1:2, :] = fac_v[0, 7:8, :]
        for place, has in ((0, has_a), (1, has_b)):
            @pl.when(has & (ahead < STEPS))
            def _():
                corner(ahead, place).start()

        for has, index, there in (
            (has_hx, 0, in_xe), (has_lx, 3, in_xh), (has_hz, 1, in_ze), (has_lz, 4, in_zh), (has_hx, 2, in_xr),
        ):
            @pl.when(has)
            def _():
                copy(index, there.at[slot], to_lx, there.at[slot], index).wait_recv()
        for has, item in (
            (has_lx, out_lx), (has_lz, out_lz), (has_lx, out_rx), (has_hx, out_hx), (has_hz, out_hz)
        ):
            @pl.when(has)
            def _():
                item.wait_send()
        for place, has_to, has_from in ((0, has_a, has_b), (1, has_b, has_a)):
            @pl.when(has_from)
            def _():
                corner(n, place).wait_recv()

            @pl.when(has_to)
            def _():
                corner(n, place).wait_send()
        here = lax.rem(n, 4)
        corner_ex = in_c[here, 0, 0:1, :] + in_c[here, 0, 1:2, :] * mix[0:1, :]
        corner_ez = in_c[here, 1, 0:1, :] + in_c[here, 1, 1:2, :] * mix[1:2, :]

        ex, ey, ez = state[0, 0], state[1, 0], state[2, 0]
        corner_x = jnp.where(top_row, wide_row(corner_ex), 0.0)
        before_y = keep_lx * (in_xh[slot, 0] + s * ez - s * corner_x)
        before_z = keep_lx * (in_xh[slot, 1] - s * ey)
        face = in_ze[slot, 1, 0:1, :]
        mix[0:1, :] = before_y[7:8, :] - s * (face - prev_row(face)) - s * in_ze[slot, 0, wide : wide + 1, :]
        for x in range(wide):
            ex, ey, ez = state[0, x], state[1, x], state[2, x]
            above_x = wide_row(in_ze[slot, 0, x : x + 1, :])
            above_y = wide_row(in_ze[slot, 1, x : x + 1, :])
            hx = state[3, x] + jnp.where(top_row, s * above_y, 0.0)
            hy = state[4, x] - jnp.where(top_row, s * above_x, 0.0)
            hz = state[5, x]
            below_x = wide_row(in_zh[slot, 0, x : x + 1, :]) + s * ey
            below_y = wide_row(in_zh[slot, 1, x : x + 1, :]) - s * ex
            if x == last:
                hy = hy + s * in_xe[slot, 1]
                hz = hz - s * in_xe[slot, 0]
                below_y = below_y + s * wide_row(corner_ez)
                face = in_xe[slot, 0, 0:1, :]
                mix[1:2, :] = -below_y[0:1, :] - s * in_xr[slot] - s * (face - prev_row(face))
            down_x = jnp.where(first_row, keep_lz * below_x, pltpu.roll(hx, 1, 0))
            down_y = jnp.where(first_row, keep_lz * below_y, pltpu.roll(hy, 1, 0))
            fac = fac_v[x]
            state[0, x] = ex + fac * ((hz - prev_y(hz)) - (hy - down_y)) + src_v[x] * pulse
            state[1, x] = ey + fac * ((hx - down_x) - (hz - before_z))
            state[2, x] = ez + fac * ((hy - before_y) - (hx - prev_y(hx)))
            state[3, x] = hx
            state[4, x] = hy
            state[5, x] = hz
            before_y, before_z = hy, hz

        @pl.when(at_exit)
        def _():
            for x in range(wide):
                rows_top[0, x : x + 1, :] = state[0, x, 7:8, :]
                rows_top[1, x : x + 1, :] = state[1, x, 7:8, :]
            for f in range(2):
                for part in range(2):
                    weight = turn_ref[4 * n + 2 * f + part]
                    for c in range(2):
                        spec[4 * f + 2 * c + part] += weight * rows_top[c]

        return carry

    lax.fori_loop(0, STEPS, one_step, 0)

    lane_group = lax.broadcasted_iota(jnp.int32, (8, 128), 1) // 8
    half = planes.shape[1] // 2

    def place_plane(index, value, lanes):
        f, c, part = index // 4, index // 2 % 2, index % 2
        base = 32 * f + 16 * c
        if part == 0:
            planes[base : base + 8, pl.ds(lanes, value.shape[1])] = value
            planes[base + 8 : base + 16, pl.ds(half + lanes, value.shape[1])] = value
        else:
            planes[base : base + 8, pl.ds(half + lanes, value.shape[1])] = -value
            planes[base + 8 : base + 16, pl.ds(lanes, value.shape[1])] = value

    def transform(high, low, result):
        total = None
        for f in range(2):
            value = planes[...]
            mine = lax.broadcasted_iota(jnp.int32, value.shape, 0) // 32 == f
            value = jnp.where(mine, value, 0.0)
            upper = value.astype(jnp.bfloat16)
            lower = (value - upper.astype(jnp.float32)).astype(jnp.bfloat16)
            right = jnp.concatenate([upper, lower], axis=0)
            dims = (((1,), (1,)), ((), ()))
            first = lax.dot_general(high[f], right, dims, preferred_element_type=jnp.float32)
            second = lax.dot_general(low[f], right, dims, preferred_element_type=jnp.float32)
            part = first + pltpu.roll(first, 64, 1) + second
            total = part if total is None else total + part
        result[...] = total

    def tile(ref, index):
        return ref.at[pl.ds(pl.multiple_of(8 * index, 8), 8), :]

    @pl.when(at_exit)
    def _():
        for item in tables:
            item.wait()
        for index in range(8):
            place_plane(index, spec[index], 0)
        transform(col_high, col_low, out_a)

        def send_a(i, carry):
            peer = lax.rem(pos_x + i, count_x)
            pltpu.make_async_remote_copy(
                src_ref=tile(out_a, peer), dst_ref=in_a.at[pos_x], send_sem=tail_send.at[0],
                recv_sem=tail_recv.at[0], device_id=(exit_z, peer), device_id_type=MESH,
            ).start()
            return carry

        lax.fori_loop(1, count_x, send_a, 0)
        in_a[pos_x] = out_a[pl.ds(pl.multiple_of(8 * pos_x, 8), 8), :]
        others = in_a.at[pl.ds(0, count_x - 1)]
        whole = pltpu.make_async_remote_copy(
            src_ref=others, dst_ref=others, send_sem=tail_send.at[0], recv_sem=tail_recv.at[0],
            device_id=(exit_z, pos_x), device_id_type=MESH,
        )
        whole.wait_recv()
        whole.wait_send()
        for block in range(count_x // 16):
            values = [in_a[16 * block + j] for j in range(16)]
            for index in range(8):
                lined = jnp.zeros((8, 128), jnp.float32)
                for j in range(16):
                    moved = pltpu.roll(values[j], (8 * (j - index)) % 128, 1) if j != index else values[j]
                    lined = jnp.where(lane_group == j, moved, lined)
                place_plane(index, lined, 128 * block)
        transform(row_high, row_low, out_b)
        mine = lax.rem(pos_x, group)

        def send_b(i, carry):
            peer = lax.rem(pos_x + i, count_x)
            pltpu.make_async_remote_copy(
                src_ref=tile(out_b, peer), dst_ref=in_b.at[mine], send_sem=tail_send.at[1],
                recv_sem=tail_recv.at[1], device_id=(target_z, peer), device_id_type=MESH,
            ).start()
            return carry

        lax.fori_loop(1, count_x, send_b, 0)

        @pl.when(target_z != exit_z)
        def _():
            send_b(0, 0)

        @pl.when(target_z == exit_z)
        def _():
            in_b[mine] = out_b[pl.ds(pl.multiple_of(8 * pos_x, 8), 8), :]

    def arrived(number):
        return pltpu.make_async_remote_copy(
            src_ref=in_a.at[pl.ds(0, number)], dst_ref=in_b.at[pl.ds(0, number)], send_sem=tail_send.at[1],
            recv_sem=tail_recv.at[1], device_id=(exit_z, pos_x), device_id_type=MESH,
        )

    own = at_exit & (target_z == exit_z)

    @pl.when(own)
    def _():
        arrived(group - 1).wait_recv()

    @pl.when(jnp.logical_not(own))
    def _():
        arrived(group).wait_recv()

    columns = image.shape[2]
    values = [in_b[j] for j in range(group)]
    for index in range(8):
        lined = jnp.zeros((8, 128), jnp.float32)
        for j in range(group):
            moved = pltpu.roll(values[j], (8 * (j - index)) % 128, 1) if j != index else values[j]
            lined = jnp.where(lane_group == j, moved, lined)
        image[:, index, :] = lined[:wide, :columns]

    def sent(number):
        return pltpu.make_async_remote_copy(
            src_ref=in_a.at[pl.ds(0, number)], dst_ref=in_a.at[pl.ds(0, number)], send_sem=tail_send.at[1],
            recv_sem=tail_recv.at[1], device_id=(exit_z, pos_x), device_id_type=MESH,
        )

    @pl.when(own)
    def _():
        sent(count_x - 1).wait_send()

    @pl.when(at_exit & jnp.logical_not(own))
    def _():
        sent(count_x).wait_send()


def march(count_z, count_x, fields, material, mask, eps_table, kerr_table):
    _, wide, deep, span = fields.shape
    vmem = pl.BlockSpec(memory_space=pltpu.VMEM)
    f32 = jnp.float32
    tables = chirp(span, span) + chirp(count_x * wide, wide)
    return pl.pallas_call(
        functools.partial(step_kernel, count_z, count_x),
        out_shape=(
            jax.ShapeDtypeStruct(fields.shape, f32),
            jax.ShapeDtypeStruct((wide, 8, span // count_z), f32),
        ),
        in_specs=[pl.BlockSpec(memory_space=pl.ANY)] * 9,
        out_specs=(vmem, vmem),
        scratch_shapes=[
            pltpu.VMEM((8, 8, span), f32),
            *(pltpu.VMEM(table.shape, jnp.bfloat16) for table in tables),
            pltpu.SemaphoreType.DMA((4,)),
            pltpu.VMEM((64, 2 * max(span, 8 * count_x)), f32),
            pltpu.VMEM((span, 128), f32),
            pltpu.VMEM((count_x, 8, 128), f32),
            pltpu.VMEM((8 * count_x, 128), f32),
            pltpu.VMEM((count_x // count_z, 8, 128), f32),
            pltpu.SemaphoreType.DMA((2,)),
            pltpu.SemaphoreType.DMA((2,)),
            pltpu.VMEM((wide, deep, span), jnp.int32),
            pltpu.VMEM((wide, deep, span), jnp.int32),
            pltpu.SMEM(eps_table.shape, f32),
            pltpu.SMEM(kerr_table.shape, f32),
            pltpu.SMEM((STEPS,), f32),
            pltpu.SMEM((4 * STEPS,), f32),
            pltpu.SemaphoreType.DMA((5,)),
            pltpu.VMEM((wide, deep, span), f32),
            pltpu.VMEM((wide, deep, span), f32),
            pltpu.VMEM((wide, deep, span), f32),
            pltpu.VMEM((wide, deep, span), f32),
            pltpu.VMEM((2, wide + 1, span), f32),
            pltpu.VMEM((2, wide, span), f32),
            pltpu.VMEM((2, 8, span), f32),
            pltpu.VMEM((2, 2, 2, span), f32),
            pltpu.VMEM((2, span), f32),
            pltpu.VMEM((2, 2, deep, span), f32),
            pltpu.VMEM((2, 1, span), f32),
            pltpu.VMEM((2, 2, deep, span), f32),
            pltpu.VMEM((2, 2, wide + 1, span), f32),
            pltpu.VMEM((2, 2, wide, span), f32),
            pltpu.VMEM((4, 2, 2, span), f32),
            pltpu.SemaphoreType.DMA((5,)),
            pltpu.SemaphoreType.DMA((2, 5)),
            pltpu.SemaphoreType.DMA((2, 2)),
            pltpu.SemaphoreType.DMA((4, 2)),
        ],
        compiler_params=pltpu.CompilerParams(
            collective_id=1, has_side_effects=True, vmem_limit_bytes=60 * 1024 * 1024
        ),
        name="march",
    )(fields, material, mask, eps_table, kerr_table, *(jnp.asarray(table) for table in tables))


def local(fields, material, source_mask, eps_table, kerr_table):
    count_x, count_z = lax.axis_size("lat"), lax.axis_size("depth")
    return march(count_z, count_x, fields, material, source_mask, eps_table, kerr_table)


def solution(mesh):
    placed = (P(None, "lat", "depth", None), P("lat", "depth", None), P("lat", "depth", None), P(), P())
    return jax.shard_map(
        local, mesh=mesh, in_specs=placed,
        out_specs=(P(None, "lat", "depth", None), P("lat", None, "depth")), check_vma=False,
    )
```

```python
import functools
import math

import jax
import jax.numpy as jnp
import numpy as np
from jax import lax
from jax.experimental import pallas as pl
from jax.experimental.pallas import tpu as pltpu
from jax.sharding import PartitionSpec as P

STEPS = 16
COURANT = 0.55
OMEGAS = (0.9, 1.3)
QUARTERS = (3, 5)
MESH = pl.DeviceIdType.MESH


def pulses():
    middle = np.arange(STEPS) + 0.5
    return np.asarray(np.sin(OMEGAS[0] * middle) + np.sin(OMEGAS[1] * middle), np.float32)


def turns():
    later = np.arange(STEPS) + 1.0
    parts = []
    for omega in OMEGAS:
        parts += [np.cos(omega * later), -np.sin(omega * later)]
    return np.asarray(np.stack(parts, axis=1), np.float32)


def split(table):
    high = table.astype(jnp.bfloat16)
    return high, (table - high.astype(np.float32)).astype(jnp.bfloat16)


def chirp(length, run):
    gap = np.arange(length)[:, None] - np.arange(length)[None, :]
    padded = -(-run // 8) * 8
    tables = []
    for quarter in QUARTERS:
        phase = (quarter * gap * gap % (8 * length)) * (math.pi / (4.0 * length))
        table = np.stack([np.cos(phase), np.sin(phase)], axis=1) / math.sqrt(length)
        table = table.reshape(length // run, run, 2, length // run, run)
        table = np.pad(table, ((0, 0), (0, padded - run), (0, 0), (0, 0), (0, padded - run)))
        tables.append(table.reshape(length // run * padded, 2 * (length // run) * padded))
    return split(np.asarray(np.stack(tables), np.float32))


def step_kernel(
    count_z, count_x,
    fields_hbm, material_hbm, mask_hbm, eps_hbm, kerr_hbm, col_high_hbm, col_low_hbm, row_high_hbm, row_low_hbm,
    state, image,
    spec, col_high, col_low, row_high, row_low, table_sem, planes, out_a, in_a, out_b, in_b, tail_send, tail_recv,
    material_ref, mask_ref, eps_ref, kerr_ref, pulse_ref, turn_ref, load_sem,
    eps_v, kerr_v, src_v, fac_v,
    rows_e, rows_h, rows_top, corner_s, mix,
    in_all, in_c, send_sem, recv_sem, corner_send, corner_recv,
):
    wide = state.shape[1]
    span = state.shape[3]
    last = wide - 1
    pos_z = lax.axis_index("depth")
    pos_x = lax.axis_index("lat")
    has_lx, has_hx = pos_x > 0, pos_x < count_x - 1
    has_lz, has_hz = pos_z > 0, pos_z < count_z - 1
    has_a, has_b = has_lz & has_hx, has_hz & has_lx
    low_x, high_x, low_z, high_z = pos_x - 1, pos_x + 1, pos_z - 1, pos_z + 1
    to_lx, to_hx = (pos_z, low_x), (pos_z, high_x)
    to_lz, to_hz = (low_z, pos_x), (high_z, pos_x)
    to_a, to_b = (low_z, high_x), (high_z, low_x)
    neighbours = (
        (has_lx, to_lx), (has_hx, to_hx), (has_lz, to_lz), (has_hz, to_hz), (has_a, to_a), (has_b, to_b)
    )

    loads = [
        pltpu.make_async_copy(source, there, load_sem.at[i])
        for i, (source, there) in enumerate((
            (material_hbm, material_ref), (mask_hbm, mask_ref), (eps_hbm, eps_ref), (kerr_hbm, kerr_ref),
            (fields_hbm, state),
        ))
    ]
    for item in loads:
        item.start()
    mix[...] = jnp.zeros_like(mix)
    in_all[...] = jnp.zeros_like(in_all)
    in_c[...] = jnp.zeros_like(in_c)

    def begin(has, item):
        @pl.when(has)
        def _():
            item.start()

    def for_peers(act):
        side = 4 if count_x == 64 else 2
        runs = count_x // (side * side)
        x, z, y = pos_x // (side * runs), pos_x // side % runs, pos_x % side
        order = (2, 1, 3, 0) if side == 4 else (1, 0)
        at_x = [lax.rem(x + far, side) * (side * runs) for far in order]
        at_y = [lax.rem(y + far, side) for far in order]

        def run(k, carry):
            at_z = jnp.where(z < runs // 2, runs - 1 - k, k) * side
            for i in range(side):
                for j in range(side):
                    act(at_x[i] + at_z + at_y[j], i == side - 1 and j == side - 1)
            return carry

        lax.fori_loop(0, runs, run, 0)

    barrier = pltpu.get_barrier_semaphore()
    for has, target in neighbours:
        @pl.when(has)
        def _():
            pl.semaphore_signal(barrier, inc=1, device_id=target, device_id_type=MESH)

    exit_z = count_z - 1
    at_exit = pos_z == exit_z
    group = count_x // count_z
    for j in range(group):
        sender = pos_z * group + j
        @pl.when(jnp.logical_not(at_exit & (sender == pos_x)))
        def _():
            pl.semaphore_signal(barrier, inc=1, device_id=(exit_z, sender), device_id_type=MESH)

    tables = [
        pltpu.make_async_copy(source, there, table_sem.at[i])
        for i, (source, there) in enumerate((
            (col_high_hbm, col_high), (col_low_hbm, col_low), (row_high_hbm, row_high), (row_low_hbm, row_low)
        ))
    ]

    @pl.when(at_exit)
    def _():
        def greet(peer, may_be_own):
            def signal():
                pl.semaphore_signal(barrier, inc=1, device_id=(exit_z, peer), device_id_type=MESH)

            pl.when(peer != pos_x)(signal) if may_be_own else signal()

        for_peers(greet)
        for item in tables:
            item.start()

    for n in range(STEPS):
        pulse_ref[n] = jnp.float32(pulses()[n])
        for i in range(4):
            turn_ref[4 * n + 4 + i] = jnp.float32(turns()[n, i])
    for i in range(4):
        turn_ref[i] = jnp.float32(0.0)
    for item in loads:
        item.wait()
    material = material_ref[...]
    eps, kerr = jnp.zeros(material.shape, jnp.float32), jnp.zeros(material.shape, jnp.float32)
    for level in range(eps_ref.shape[0]):
        eps = jnp.where(material == level, eps_ref[level], eps)
        kerr = jnp.where(material == level, kerr_ref[level], kerr)
    eps_v[...] = eps
    kerr_v[...] = kerr
    src_v[...] = mask_ref[...].astype(jnp.float32)
    spec[...] = jnp.zeros_like(spec)
    rows_top[...] = jnp.zeros_like(rows_top)

    target_z = pos_x // group
    greeted = sum(jnp.where(has, 1, 0) for has, _ in neighbours)
    greeted += jnp.where(at_exit, 2 * count_x - 1 - jnp.where(target_z == exit_z, 1, 0), 0)
    pl.semaphore_wait(barrier, greeted)

    row = lax.broadcasted_iota(jnp.int32, (8, span), 0)
    col = lax.broadcasted_iota(jnp.int32, (8, span), 1)
    top_row, first_row = row == 7, row == 0
    top_col, first_col = col == span - 1, col == 0
    s = jnp.float32(COURANT)
    keep_lx = jnp.where(has_lx, 1.0, 0.0).astype(jnp.float32)
    keep_lz = jnp.where(has_lz, 1.0, 0.0).astype(jnp.float32)
    keep_hx = jnp.where(has_hx, 1.0, 0.0).astype(jnp.float32)
    keep_hz = jnp.where(has_hz, 1.0, 0.0).astype(jnp.float32)

    def next_y(f):
        return jnp.where(top_col, 0.0, pltpu.roll(f, span - 1, 1))

    def prev_y(f):
        return jnp.where(first_col, 0.0, pltpu.roll(f, 1, 1))

    def next_z(f):
        return jnp.where(top_row, 0.0, pltpu.roll(f, 7, 0))

    def wide_row(r):
        return jnp.broadcast_to(r, (8, span))

    def prev_row(r):
        return jnp.where(first_col[0:1], 0.0, pltpu.roll(r, 1, 1))

    def corner(when, place):
        return pltpu.make_async_remote_copy(
            src_ref=corner_s.at[lax.rem(when, 2), place], dst_ref=in_c.at[lax.rem(when, 4), place],
            send_sem=corner_send.at[lax.rem(when, 2), place], recv_sem=corner_recv.at[lax.rem(when, 4), place],
            device_id=(to_a, to_b)[place], device_id_type=MESH,
        )

    corner_s[...] = jnp.zeros_like(corner_s)
    corner_s[0, 0, 0:1, :] = state[0, last, 0:1, :]
    corner_s[0, 1, 0:1, :] = state[2, 0, 7:8, :]
    begin(has_a, corner(0, 0))
    begin(has_b, corner(0, 1))

    half = wide // 2

    def keep_rows(x, ex, ey, ez):
        part, place = x // half, x % half
        rows_e[part, place : place + 1, :] = ex[0:1, :]
        rows_e[part, half + place : half + place + 1, :] = ey[0:1, :]
        if x == 0:
            rows_e[0, 2 * half : 2 * half + 1, :] = ez[0:1, :]

    def advance_h(x):
        ex, ey, ez = state[0, x], state[1, x], state[2, x]
        if x < last:
            ahead_y, ahead_z = state[1, x + 1], state[2, x + 1]
        else:
            ahead_y, ahead_z = jnp.zeros_like(ey), jnp.zeros_like(ez)
        hx = state[3, x] - s * ((next_y(ez) - ez) - (next_z(ey) - ey))
        hy = state[4, x] - s * ((next_z(ex) - ex) - (ahead_z - ez))
        hz = state[5, x] - s * ((ahead_y - ey) - (next_y(ex) - ex))
        state[3, x] = hx
        state[4, x] = hy
        state[5, x] = hz
        part, place = x // half, x % half
        rows_h[part, place : place + 1, :] = hx[7:8, :]
        rows_h[part, half + place : half + place + 1, :] = hy[7:8, :]

    def copies(n):
        slot = lax.rem(n, 2)

        def copy(index, source, target, there):
            return pltpu.make_async_remote_copy(
                src_ref=source, dst_ref=there, send_sem=send_sem.at[index], recv_sem=recv_sem.at[slot, index],
                device_id=target, device_id_type=MESH,
            )

        first, second = slice(0, 2 * half + 1), slice(0, 2 * half)
        return {
            "xe": (copy(0, state.at[1:3, 0], to_lx, in_all.at[slot, 0:2]), has_lx, has_hx),
            "xr": (copy(1, rows_e.at[0, 0:1], to_lx, in_all.at[slot, 8, 0:1]), has_lx, has_hx),
            "xh": (copy(2, state.at[4:6, last], to_hx, in_all.at[slot, 2:4]), has_hx, has_lx),
            "ze0": (copy(3, rows_e.at[0, first], to_lz, in_all.at[slot, 4, first]), has_lz, has_hz),
            "ze1": (copy(4, rows_e.at[1, second], to_lz, in_all.at[slot, 5, second]), has_lz, has_hz),
            "zh0": (copy(5, rows_h.at[0, second], to_hz, in_all.at[slot, 6, second]), has_hz, has_lz),
            "zh1": (copy(6, rows_h.at[1, second], to_hz, in_all.at[slot, 7, second]), has_hz, has_lz),
        }

    def send(items, *names):
        for name in names:
            item, has_to, _ = items[name]
            begin(has_to, item)

    def receive(items, *names):
        for name in names:
            item, _, has_from = items[name]
            pl.when(has_from)(item.wait_recv)

    def accumulate(n):
        for x in range(wide):
            rows_top[0, x : x + 1, :] = state[0, x, 7:8, :]
            rows_top[1, x : x + 1, :] = state[1, x, 7:8, :]
        for f in range(2):
            for part in range(2):
                weight = turn_ref[4 * n + 2 * f + part]
                for c in range(2):
                    spec[4 * f + 2 * c + part] += weight * rows_top[c]

    for x in range(wide):
        keep_rows(x, state[0, x], state[1, x], state[2, x])
    started = copies(0)
    send(started, "ze0", "ze1", "xe", "xr")
    for x in range(wide):
        advance_h(x)
    send(started, "zh0", "zh1", "xh")

    def one_step(n, more):
        slot = lax.rem(n, 2)
        now, later = copies(n), copies(n + 1) if more else {}

        @pl.when(at_exit)
        def _():
            accumulate(n)

        for x in range(wide):
            ex, ey, ez = state[0, x], state[1, x], state[2, x]
            fac_v[x] = s / (eps_v[x] + kerr_v[x] * (ex * ex + ey * ey + ez * ez))

        pulse = pulse_ref[n]
        ahead = n + 1
        side = lax.rem(ahead, 2)
        if more:
            corner_s[side, 0, 0:1, :] = (
                state[0, last, 0:1, :] + src_v[last, 0:1, :] * pulse + fac_v[last, 0:1, :]
                * (state[5, last, 0:1, :] - prev_row(state[5, last, 0:1, :]) - state[4, last, 0:1, :])
            )
            corner_s[side, 0, 1:2, :] = fac_v[last, 0:1, :]
            corner_s[side, 1, 0:1, :] = state[2, 0, 7:8, :] + fac_v[0, 7:8, :] * (
                state[4, 0, 7:8, :] - (state[3, 0, 7:8, :] - prev_row(state[3, 0, 7:8, :]))
            )
            corner_s[side, 1, 1:2, :] = fac_v[0, 7:8, :]
            begin(has_a, corner(ahead, 0))
            begin(has_b, corner(ahead, 1))

        for item, has_to, _ in now.values():
            pl.when(has_to)(item.wait_send)
        for place, has_to, has_from in ((0, has_a, has_b), (1, has_b, has_a)):
            pl.when(has_to)(corner(n, place).wait_send)
            pl.when(has_from)(corner(n, place).wait_recv)
        receive(now, "xh", "ze0", "zh0")
        here = lax.rem(n, 4)
        corner_ex = in_c[here, 0, 0:1, :] + in_c[here, 0, 1:2, :] * mix[0:1, :]
        corner_ez = in_c[here, 1, 0:1, :] + in_c[here, 1, 1:2, :] * mix[1:2, :]

        ex, ey, ez = state[0, 0], state[1, 0], state[2, 0]
        corner_x = jnp.where(top_row, wide_row(keep_hz * corner_ex), 0.0)
        before_y = keep_lx * (in_all[slot, 2] + s * ez - s * corner_x)
        before_z = keep_lx * (in_all[slot, 3] - s * ey)
        face = in_all[slot, 4, half : half + 1, :]
        mix[0:1, :] = before_y[7:8, :] - s * (face - prev_row(face)) - s * in_all[slot, 4, 2 * half : 2 * half + 1, :]
        for x in range(wide):
            part, place = x // half, x % half
            if x == half:
                receive(now, "ze1", "zh1")
            if x == last:
                receive(now, "xe", "xr")
            ex, ey, ez = state[0, x], state[1, x], state[2, x]
            above_x = wide_row(in_all[slot, 4 + part, place : place + 1, :])
            above_y = wide_row(in_all[slot, 4 + part, half + place : half + place + 1, :])
            hx = state[3, x] + jnp.where(top_row, (s * keep_hz) * above_y, 0.0)
            hy = state[4, x] - jnp.where(top_row, (s * keep_hz) * above_x, 0.0)
            hz = state[5, x]
            below_x = wide_row(in_all[slot, 6 + part, place : place + 1, :]) + s * ey
            below_y = wide_row(in_all[slot, 6 + part, half + place : half + place + 1, :]) - s * ex
            if x == last:
                hy = hy + (s * keep_hx) * in_all[slot, 1]
                hz = hz - (s * keep_hx) * in_all[slot, 0]
                below_y = below_y + s * wide_row(keep_hx * corner_ez)
                face = in_all[slot, 0, 0:1, :]
                mix[1:2, :] = -below_y[0:1, :] - s * in_all[slot, 8, 0:1, :] - s * (face - prev_row(face))
            down_x = jnp.where(first_row, keep_lz * below_x, pltpu.roll(hx, 1, 0))
            down_y = jnp.where(first_row, keep_lz * below_y, pltpu.roll(hy, 1, 0))
            fac = fac_v[x]
            ex = ex + fac * ((hz - prev_y(hz)) - (hy - down_y)) + src_v[x] * pulse
            ey = ey + fac * ((hx - down_x) - (hz - before_z))
            ez = ez + fac * ((hy - before_y) - (hx - prev_y(hx)))
            keep_rows(x, ex, ey, ez)
            state[0, x] = ex
            state[1, x] = ey
            state[2, x] = ez
            state[3, x] = hx
            state[4, x] = hy
            state[5, x] = hz
            before_y, before_z = hy, hz
            if more:
                if x == 0:
                    send(later, "xe", "xr")
                if x == half - 1:
                    send(later, "ze0")
                if x == last:
                    send(later, "ze1")
                if x > 0:
                    advance_h(x - 1)
                if x == half:
                    send(later, "zh0")
        if more:
            advance_h(last)
            send(later, "zh1", "xh")

    def full_step(n, carry):
        one_step(n, True)
        return carry

    lax.fori_loop(0, STEPS - 1, full_step, 0)
    one_step(STEPS - 1, False)

    lane_group = lax.broadcasted_iota(jnp.int32, (8, 128), 1) // 8
    middle = planes.shape[1] // 2

    def place_plane(index, value, lanes):
        f, c, part = index // 4, index // 2 % 2, index % 2
        base = 32 * f + 16 * c
        if part == 0:
            planes[base : base + 8, pl.ds(lanes, value.shape[1])] = value
            planes[base + 8 : base + 16, pl.ds(middle + lanes, value.shape[1])] = value
        else:
            planes[base : base + 8, pl.ds(middle + lanes, value.shape[1])] = -value
            planes[base + 8 : base + 16, pl.ds(lanes, value.shape[1])] = value

    def transform(high, low, result):
        total = None
        for f in range(2):
            value = planes[...]
            mine = lax.broadcasted_iota(jnp.int32, value.shape, 0) // 32 == f
            value = jnp.where(mine, value, 0.0)
            upper = value.astype(jnp.bfloat16)
            lower = (value - upper.astype(jnp.float32)).astype(jnp.bfloat16)
            right = jnp.concatenate([upper, lower], axis=0)
            dims = (((1,), (1,)), ((), ()))
            first = lax.dot_general(high[f], right, dims, preferred_element_type=jnp.float32)
            second = lax.dot_general(low[f], right, dims, preferred_element_type=jnp.float32)
            part = first + pltpu.roll(first, 64, 1) + second
            total = part if total is None else total + part
        result[...] = total

    def tile(ref, index):
        return ref.at[pl.ds(pl.multiple_of(8 * index, 8), 8), :]

    @pl.when(at_exit)
    def _():
        for item in tables:
            item.wait()
        accumulate(STEPS)
        for index in range(8):
            place_plane(index, spec[index], 0)
        transform(col_high, col_low, out_a)

        def send_a(peer, may_be_own):
            item = pltpu.make_async_remote_copy(
                src_ref=tile(out_a, peer), dst_ref=in_a.at[pos_x], send_sem=tail_send.at[0],
                recv_sem=tail_recv.at[0], device_id=(exit_z, peer), device_id_type=MESH,
            )
            begin(peer != pos_x, item) if may_be_own else item.start()

        for_peers(send_a)
        in_a[pos_x] = out_a[pl.ds(pl.multiple_of(8 * pos_x, 8), 8), :]
        others = in_a.at[pl.ds(0, count_x - 1)]
        whole = pltpu.make_async_remote_copy(
            src_ref=others, dst_ref=others, send_sem=tail_send.at[0], recv_sem=tail_recv.at[0],
            device_id=(exit_z, pos_x), device_id_type=MESH,
        )
        whole.wait_recv()
        whole.wait_send()
        for block in range(count_x // 16):
            values = [in_a[16 * block + j] for j in range(16)]
            for index in range(8):
                lined = jnp.zeros((8, 128), jnp.float32)
                for j in range(16):
                    moved = pltpu.roll(values[j], (8 * (j - index)) % 128, 1) if j != index else values[j]
                    lined = jnp.where(lane_group == j, moved, lined)
                place_plane(index, lined, 128 * block)
        transform(row_high, row_low, out_b)
        mine = lax.rem(pos_x, group)

        def send_b(peer, may_be_own):
            item = pltpu.make_async_remote_copy(
                src_ref=tile(out_b, peer), dst_ref=in_b.at[mine], send_sem=tail_send.at[1],
                recv_sem=tail_recv.at[1], device_id=(target_z, peer), device_id_type=MESH,
            )
            begin((target_z != exit_z) | (peer != pos_x), item) if may_be_own else item.start()

        for_peers(send_b)

        @pl.when(target_z == exit_z)
        def _():
            in_b[mine] = out_b[pl.ds(pl.multiple_of(8 * pos_x, 8), 8), :]

    def arrived(number):
        return pltpu.make_async_remote_copy(
            src_ref=in_a.at[pl.ds(0, number)], dst_ref=in_b.at[pl.ds(0, number)], send_sem=tail_send.at[1],
            recv_sem=tail_recv.at[1], device_id=(exit_z, pos_x), device_id_type=MESH,
        )

    own = at_exit & (target_z == exit_z)

    @pl.when(own)
    def _():
        arrived(group - 1).wait_recv()

    @pl.when(jnp.logical_not(own))
    def _():
        arrived(group).wait_recv()

    columns = image.shape[2]
    values = [in_b[j] for j in range(group)]
    for index in range(8):
        lined = jnp.zeros((8, 128), jnp.float32)
        for j in range(group):
            moved = pltpu.roll(values[j], (8 * (j - index)) % 128, 1) if j != index else values[j]
            lined = jnp.where(lane_group == j, moved, lined)
        image[:, index, :] = lined[:wide, :columns]

    def sent(number):
        return pltpu.make_async_remote_copy(
            src_ref=in_a.at[pl.ds(0, number)], dst_ref=in_a.at[pl.ds(0, number)], send_sem=tail_send.at[1],
            recv_sem=tail_recv.at[1], device_id=(exit_z, pos_x), device_id_type=MESH,
        )

    @pl.when(own)
    def _():
        sent(count_x - 1).wait_send()

    @pl.when(at_exit & jnp.logical_not(own))
    def _():
        sent(count_x).wait_send()


def march(count_z, count_x, fields, material, mask, eps_table, kerr_table):
    _, wide, deep, span = fields.shape
    vmem = pl.BlockSpec(memory_space=pltpu.VMEM)
    f32 = jnp.float32
    tables = chirp(span, span) + chirp(count_x * wide, wide)
    return pl.pallas_call(
        functools.partial(step_kernel, count_z, count_x),
        out_shape=(
            jax.ShapeDtypeStruct(fields.shape, f32),
            jax.ShapeDtypeStruct((wide, 8, span // count_z), f32),
        ),
        in_specs=[pl.BlockSpec(memory_space=pl.ANY)] * 9,
        out_specs=(vmem, vmem),
        scratch_shapes=[
            pltpu.VMEM((8, 8, span), f32),
            *(pltpu.VMEM(table.shape, jnp.bfloat16) for table in tables),
            pltpu.SemaphoreType.DMA((4,)),
            pltpu.VMEM((64, 2 * max(span, 8 * count_x)), f32),
            pltpu.VMEM((span, 128), f32),
            pltpu.VMEM((count_x, 8, 128), f32),
            pltpu.VMEM((8 * count_x, 128), f32),
            pltpu.VMEM((count_x // count_z, 8, 128), f32),
            pltpu.SemaphoreType.DMA((2,)),
            pltpu.SemaphoreType.DMA((2,)),
            pltpu.VMEM((wide, deep, span), jnp.int32),
            pltpu.VMEM((wide, deep, span), jnp.int32),
            pltpu.SMEM(eps_table.shape, f32),
            pltpu.SMEM(kerr_table.shape, f32),
            pltpu.SMEM((STEPS,), f32),
            pltpu.SMEM((4 * STEPS + 4,), f32),
            pltpu.SemaphoreType.DMA((5,)),
            pltpu.VMEM((wide, deep, span), f32),
            pltpu.VMEM((wide, deep, span), f32),
            pltpu.VMEM((wide, deep, span), f32),
            pltpu.VMEM((wide, deep, span), f32),
            pltpu.VMEM((2, 8, span), f32),
            pltpu.VMEM((2, 8, span), f32),
            pltpu.VMEM((2, 8, span), f32),
            pltpu.VMEM((2, 2, 2, span), f32),
            pltpu.VMEM((2, span), f32),
            pltpu.VMEM((2, 9, 8, span), f32),
            pltpu.VMEM((4, 2, 2, span), f32),
            pltpu.SemaphoreType.DMA((7,)),
            pltpu.SemaphoreType.DMA((2, 7)),
            pltpu.SemaphoreType.DMA((2, 2)),
            pltpu.SemaphoreType.DMA((4, 2)),
        ],
        compiler_params=pltpu.CompilerParams(
            collective_id=1, has_side_effects=True, vmem_limit_bytes=60 * 1024 * 1024
        ),
        name="march",
    )(fields, material, mask, eps_table, kerr_table, *(jnp.asarray(table) for table in tables))


def local(fields, material, source_mask, eps_table, kerr_table):
    count_x, count_z = lax.axis_size("lat"), lax.axis_size("depth")
    return march(count_z, count_x, fields, material, source_mask, eps_table, kerr_table)


def solution(mesh):
    placed = (P(None, "lat", "depth", None), P("lat", "depth", None), P("lat", "depth", None), P(), P())
    return jax.shard_map(
        local, mesh=mesh, in_specs=placed,
        out_specs=(P(None, "lat", "depth", None), P("lat", None, "depth")), check_vma=False,
    )
```

```python
import functools
import math

import jax
import jax.numpy as jnp
import numpy as np
from jax import lax
from jax.experimental import pallas as pl
from jax.experimental.pallas import tpu as pltpu
from jax.sharding import PartitionSpec as P

STEPS = 16
COURANT = 0.55
OMEGAS = (0.9, 1.3)
QUARTERS = (3, 5)
MESH = pl.DeviceIdType.MESH


def pulses():
    middle = np.arange(STEPS) + 0.5
    return np.asarray(np.sin(OMEGAS[0] * middle) + np.sin(OMEGAS[1] * middle), np.float32)


def turns():
    later = np.arange(STEPS) + 1.0
    parts = []
    for omega in OMEGAS:
        parts += [np.cos(omega * later), -np.sin(omega * later)]
    return np.asarray(np.stack(parts, axis=1), np.float32)


def split(table):
    high = table.astype(jnp.bfloat16)
    return high, (table - high.astype(np.float32)).astype(jnp.bfloat16)


def chirp(length, run):
    gap = np.arange(length)[:, None] - np.arange(length)[None, :]
    padded = -(-run // 8) * 8
    tables = []
    for quarter in QUARTERS:
        phase = (quarter * gap * gap % (8 * length)) * (math.pi / (4.0 * length))
        table = np.stack([np.cos(phase), np.sin(phase)], axis=1) / math.sqrt(length)
        table = table.reshape(length // run, run, 2, length // run, run)
        table = np.pad(table, ((0, 0), (0, padded - run), (0, 0), (0, 0), (0, padded - run)))
        tables.append(table.reshape(length // run * padded, 2 * (length // run) * padded))
    return split(np.asarray(np.stack(tables), np.float32))


def step_kernel(
    count_z, count_x,
    fields_hbm, material_hbm, mask_hbm, eps_hbm, kerr_hbm, col_high_hbm, col_low_hbm, row_high_hbm, row_low_hbm,
    fields_out, image,
    state, spec, col_high, col_low, row_high, row_low, table_sem, planes, out_a, in_a, out_b, in_b, tail_send, tail_recv,
    material_ref, mask_ref, eps_ref, kerr_ref, pulse_ref, turn_ref, load_sem,
    eps_v, kerr_v, src_v, fac_v,
    rows_e, rows_h, rows_top, corner_s, mix,
    in_all, in_c, send_sem, recv_sem, corner_send, corner_recv,
):
    wide = state.shape[1]
    span = state.shape[3]
    last = wide - 1
    pos_z = lax.axis_index("depth")
    pos_x = lax.axis_index("lat")
    has_lx, has_hx = pos_x > 0, pos_x < count_x - 1
    has_lz, has_hz = pos_z > 0, pos_z < count_z - 1
    has_a, has_b = has_lz & has_hx, has_hz & has_lx
    low_x, high_x, low_z, high_z = pos_x - 1, pos_x + 1, pos_z - 1, pos_z + 1
    to_lx, to_hx = (pos_z, low_x), (pos_z, high_x)
    to_lz, to_hz = (low_z, pos_x), (high_z, pos_x)
    to_a, to_b = (low_z, high_x), (high_z, low_x)
    neighbours = (
        (has_lx, to_lx), (has_hx, to_hx), (has_lz, to_lz), (has_hz, to_hz), (has_a, to_a), (has_b, to_b)
    )

    loads = [
        pltpu.make_async_copy(source, there, load_sem.at[i])
        for i, (source, there) in enumerate((
            (material_hbm, material_ref), (mask_hbm, mask_ref), (eps_hbm, eps_ref), (kerr_hbm, kerr_ref),
            (fields_hbm, state),
        ))
    ]
    for item in loads:
        item.start()
    mix[...] = jnp.zeros_like(mix)
    in_all[...] = jnp.zeros_like(in_all)
    in_c[...] = jnp.zeros_like(in_c)

    def begin(has, item):
        @pl.when(has)
        def _():
            item.start()

    def for_peers(act):
        side = 4 if count_x == 64 else 2
        runs = count_x // (side * side)
        x, z, y = pos_x // (side * runs), pos_x // side % runs, pos_x % side
        order = (2, 1, 3, 0) if side == 4 else (1, 0)
        at_x = [lax.rem(x + far, side) * (side * runs) for far in order]
        at_y = [lax.rem(y + far, side) for far in order]

        def run(k, carry):
            at_z = jnp.where(z < runs // 2, runs - 1 - k, k) * side
            for i in range(side):
                for j in range(side):
                    act(at_x[i] + at_z + at_y[j], i == side - 1 and j == side - 1)
            return carry

        lax.fori_loop(0, runs, run, 0)

    barrier = pltpu.get_barrier_semaphore()
    exit_z = count_z - 1
    at_exit = pos_z == exit_z
    group = count_x // count_z
    for j in range(group):
        sender = pos_z * group + j
        @pl.when(jnp.logical_not(at_exit & (sender == pos_x)))
        def _():
            pl.semaphore_signal(barrier, inc=1, device_id=(exit_z, sender), device_id_type=MESH)

    tables = [
        pltpu.make_async_copy(source, there, table_sem.at[i])
        for i, (source, there) in enumerate((
            (col_high_hbm, col_high), (col_low_hbm, col_low), (row_high_hbm, row_high), (row_low_hbm, row_low)
        ))
    ]

    @pl.when(at_exit)
    def _():
        def greet(peer, may_be_own):
            def signal():
                pl.semaphore_signal(barrier, inc=1, device_id=(exit_z, peer), device_id_type=MESH)

            pl.when(peer != pos_x)(signal) if may_be_own else signal()

        for_peers(greet)

    for has, target in neighbours:
        @pl.when(has)
        def _():
            pl.semaphore_signal(barrier, inc=1, device_id=target, device_id_type=MESH)

    @pl.when(at_exit)
    def _():
        for item in tables:
            item.start()

    for n in range(STEPS):
        pulse_ref[n] = jnp.float32(pulses()[n])
        for i in range(4):
            turn_ref[4 * n + 4 + i] = jnp.float32(turns()[n, i])
    for i in range(4):
        turn_ref[i] = jnp.float32(0.0)
    for item in loads:
        item.wait()
    material = material_ref[...]
    eps, kerr = jnp.zeros(material.shape, jnp.float32), jnp.zeros(material.shape, jnp.float32)
    for level in range(eps_ref.shape[0]):
        eps = jnp.where(material == level, eps_ref[level], eps)
        kerr = jnp.where(material == level, kerr_ref[level], kerr)
    eps_v[...] = eps
    kerr_v[...] = kerr
    src_v[...] = mask_ref[...].astype(jnp.float32)
    spec[...] = jnp.zeros_like(spec)
    rows_top[...] = jnp.zeros_like(rows_top)

    target_z = pos_x // group
    greeted = sum(jnp.where(has, 1, 0) for has, _ in neighbours)
    greeted += jnp.where(at_exit, 2 * count_x - 1 - jnp.where(target_z == exit_z, 1, 0), 0)
    pl.semaphore_wait(barrier, greeted)

    row = lax.broadcasted_iota(jnp.int32, (8, span), 0)
    col = lax.broadcasted_iota(jnp.int32, (8, span), 1)
    top_row, first_row = row == 7, row == 0
    top_col, first_col = col == span - 1, col == 0
    s = jnp.float32(COURANT)
    keep_lx = jnp.where(has_lx, 1.0, 0.0).astype(jnp.float32)
    keep_lz = jnp.where(has_lz, 1.0, 0.0).astype(jnp.float32)
    keep_hx = jnp.where(has_hx, 1.0, 0.0).astype(jnp.float32)
    keep_hz = jnp.where(has_hz, 1.0, 0.0).astype(jnp.float32)

    def next_y(f):
        return jnp.where(top_col, 0.0, pltpu.roll(f, span - 1, 1))

    def prev_y(f):
        return jnp.where(first_col, 0.0, pltpu.roll(f, 1, 1))

    def next_z(f):
        return jnp.where(top_row, 0.0, pltpu.roll(f, 7, 0))

    def wide_row(r):
        return jnp.broadcast_to(r, (8, span))

    def prev_row(r):
        return jnp.where(first_col[0:1], 0.0, pltpu.roll(r, 1, 1))

    def corner(when, place):
        return pltpu.make_async_remote_copy(
            src_ref=corner_s.at[lax.rem(when, 2), place], dst_ref=in_c.at[lax.rem(when, 4), place],
            send_sem=corner_send.at[lax.rem(when, 2), place], recv_sem=corner_recv.at[lax.rem(when, 4), place],
            device_id=(to_a, to_b)[place], device_id_type=MESH,
        )

    corner_s[...] = jnp.zeros_like(corner_s)
    corner_s[0, 0, 0:1, :] = state[0, last, 0:1, :]
    corner_s[0, 1, 0:1, :] = state[2, 0, 7:8, :]
    begin(has_a, corner(0, 0))
    begin(has_b, corner(0, 1))

    half = wide // 2

    def keep_rows(x, ex, ey, ez):
        part, place = x // half, x % half
        rows_e[part, place : place + 1, :] = ex[0:1, :]
        rows_e[part, half + place : half + place + 1, :] = ey[0:1, :]
        if x == 0:
            rows_e[0, 2 * half : 2 * half + 1, :] = ez[0:1, :]

    def advance_h(x):
        ex, ey, ez = state[0, x], state[1, x], state[2, x]
        if x < last:
            ahead_y, ahead_z = state[1, x + 1], state[2, x + 1]
        else:
            ahead_y, ahead_z = jnp.zeros_like(ey), jnp.zeros_like(ez)
        hx = state[3, x] - s * ((next_y(ez) - ez) - (next_z(ey) - ey))
        hy = state[4, x] - s * ((next_z(ex) - ex) - (ahead_z - ez))
        hz = state[5, x] - s * ((ahead_y - ey) - (next_y(ex) - ex))
        state[3, x] = hx
        state[4, x] = hy
        state[5, x] = hz
        part, place = x // half, x % half
        rows_h[part, place : place + 1, :] = hx[7:8, :]
        rows_h[part, half + place : half + place + 1, :] = hy[7:8, :]

    def copies(n):
        slot = lax.rem(n, 2)

        def copy(index, source, target, there):
            return pltpu.make_async_remote_copy(
                src_ref=source, dst_ref=there, send_sem=send_sem.at[index], recv_sem=recv_sem.at[slot, index],
                device_id=target, device_id_type=MESH,
            )

        first, second = slice(0, 2 * half + 1), slice(0, 2 * half)
        return {
            "xe": (copy(0, state.at[1:3, 0], to_lx, in_all.at[slot, 0:2]), has_lx, has_hx),
            "xr": (copy(1, rows_e.at[0, 0:1], to_lx, in_all.at[slot, 8, 0:1]), has_lx, has_hx),
            "xh": (copy(2, state.at[4:6, last], to_hx, in_all.at[slot, 2:4]), has_hx, has_lx),
            "ze0": (copy(3, rows_e.at[0, first], to_lz, in_all.at[slot, 4, first]), has_lz, has_hz),
            "ze1": (copy(4, rows_e.at[1, second], to_lz, in_all.at[slot, 5, second]), has_lz, has_hz),
            "zh0": (copy(5, rows_h.at[0, second], to_hz, in_all.at[slot, 6, second]), has_hz, has_lz),
            "zh1": (copy(6, rows_h.at[1, second], to_hz, in_all.at[slot, 7, second]), has_hz, has_lz),
        }

    def send(items, *names):
        for name in names:
            item, has_to, _ = items[name]
            begin(has_to, item)

    def receive(items, *names):
        for name in names:
            item, _, has_from = items[name]
            pl.when(has_from)(item.wait_recv)

    def accumulate(n):
        for x in range(wide):
            rows_top[0, x : x + 1, :] = state[0, x, 7:8, :]
            rows_top[1, x : x + 1, :] = state[1, x, 7:8, :]
        for f in range(2):
            for part in range(2):
                weight = turn_ref[4 * n + 2 * f + part]
                for c in range(2):
                    spec[4 * f + 2 * c + part] += weight * rows_top[c]

    for x in range(wide):
        keep_rows(x, state[0, x], state[1, x], state[2, x])
    started = copies(0)
    send(started, "ze0", "ze1", "xe", "xr")
    for x in range(wide):
        advance_h(x)
    send(started, "zh0", "zh1", "xh")

    def one_step(n, more):
        slot = lax.rem(n, 2)
        now, later = copies(n), copies(n + 1) if more else {}

        @pl.when(at_exit)
        def _():
            accumulate(n)

        for x in range(wide):
            ex, ey, ez = state[0, x], state[1, x], state[2, x]
            fac_v[x] = s / (eps_v[x] + kerr_v[x] * (ex * ex + ey * ey + ez * ez))

        pulse = pulse_ref[n]
        ahead = n + 1
        side = lax.rem(ahead, 2)
        if more:
            corner_s[side, 0, 0:1, :] = (
                state[0, last, 0:1, :] + src_v[last, 0:1, :] * pulse + fac_v[last, 0:1, :]
                * (state[5, last, 0:1, :] - prev_row(state[5, last, 0:1, :]) - state[4, last, 0:1, :])
            )
            corner_s[side, 0, 1:2, :] = fac_v[last, 0:1, :]
            corner_s[side, 1, 0:1, :] = state[2, 0, 7:8, :] + fac_v[0, 7:8, :] * (
                state[4, 0, 7:8, :] - (state[3, 0, 7:8, :] - prev_row(state[3, 0, 7:8, :]))
            )
            corner_s[side, 1, 1:2, :] = fac_v[0, 7:8, :]
            begin(has_a, corner(ahead, 0))
            begin(has_b, corner(ahead, 1))

        for item, has_to, _ in now.values():
            pl.when(has_to)(item.wait_send)
        def complete_z(x):
            part, place = x // half, x % half
            above_x = wide_row(in_all[slot, 4 + part, place : place + 1, :])
            above_y = wide_row(in_all[slot, 4 + part, half + place : half + place + 1, :])
            hx = state[3, x] + jnp.where(top_row, (s * keep_hz) * above_y, 0.0)
            hy = state[4, x] - jnp.where(top_row, (s * keep_hz) * above_x, 0.0)
            return hx, hy, state[5, x]

        def advance_e(x, magnetic, before_y, before_z, corner_row):
            part, place = x // half, x % half
            hx, hy, hz = magnetic
            ex, ey, ez = state[0, x], state[1, x], state[2, x]
            below_x = wide_row(in_all[slot, 6 + part, place : place + 1, :]) + s * ey
            below_y = wide_row(in_all[slot, 6 + part, half + place : half + place + 1, :]) - s * ex
            if x == last:
                hy = hy + (s * keep_hx) * in_all[slot, 1]
                hz = hz - (s * keep_hx) * in_all[slot, 0]
                below_y = below_y + s * wide_row(keep_hx * corner_row)
                face = in_all[slot, 0, 0:1, :]
                mix[1:2, :] = -below_y[0:1, :] - s * in_all[slot, 8, 0:1, :] - s * (face - prev_row(face))
            down_x = jnp.where(first_row, keep_lz * below_x, pltpu.roll(hx, 1, 0))
            down_y = jnp.where(first_row, keep_lz * below_y, pltpu.roll(hy, 1, 0))
            fac = fac_v[x]
            ex = ex + fac * ((hz - prev_y(hz)) - (hy - down_y)) + src_v[x] * pulse
            ey = ey + fac * ((hx - down_x) - (hz - before_z))
            ez = ez + fac * ((hy - before_y) - (hx - prev_y(hx)))
            keep_rows(x, ex, ey, ez)
            state[0, x] = ex
            state[1, x] = ey
            state[2, x] = ez
            state[3, x] = hx
            state[4, x] = hy
            state[5, x] = hz

        receive(now, "ze0", "zh0")
        first_h = complete_z(0)
        before = first_h
        for x in range(1, last):
            if x == half:
                receive(now, "ze1", "zh1")
            magnetic = complete_z(x)
            advance_e(x, magnetic, before[1], before[2], None)
            before = magnetic
            if more and x > 1:
                advance_h(x - 1)

        for place, has_to, has_from in ((0, has_a, has_b), (1, has_b, has_a)):
            pl.when(has_to)(corner(n, place).wait_send)
            pl.when(has_from)(corner(n, place).wait_recv)
        here = lax.rem(n, 4)
        corner_ex = in_c[here, 0, 0:1, :] + in_c[here, 0, 1:2, :] * mix[0:1, :]
        corner_ez = in_c[here, 1, 0:1, :] + in_c[here, 1, 1:2, :] * mix[1:2, :]
        receive(now, "xe", "xr")
        advance_e(last, complete_z(last), before[1], before[2], corner_ez)
        if more:
            advance_h(last)
            send(later, "xh")
        receive(now, "xh")
        ex, ey, ez = state[0, 0], state[1, 0], state[2, 0]
        corner_x = jnp.where(top_row, wide_row(keep_hz * corner_ex), 0.0)
        before_y = keep_lx * (in_all[slot, 2] + s * ez - s * corner_x)
        before_z = keep_lx * (in_all[slot, 3] - s * ey)
        face = in_all[slot, 4, half : half + 1, :]
        mix[0:1, :] = (
            before_y[7:8, :] - s * (face - prev_row(face)) - s * in_all[slot, 4, 2 * half : 2 * half + 1, :]
        )
        advance_e(0, first_h, before_y, before_z, None)
        if more:
            send(later, "xe", "xr", "ze0")
        if more:
            send(later, "ze1")
            advance_h(0)
            send(later, "zh0")
            advance_h(last - 1)
            send(later, "zh1")

    def full_step(n, carry):
        one_step(n, True)
        return carry

    lax.fori_loop(0, STEPS - 1, full_step, 0)
    one_step(STEPS - 1, False)
    leave = pltpu.make_async_copy(state, fields_out, load_sem.at[0])
    leave.start()

    lane_group = lax.broadcasted_iota(jnp.int32, (8, 128), 1) // 8
    middle = planes.shape[1] // 2

    def place_plane(index, value, lanes):
        f, c, part = index // 4, index // 2 % 2, index % 2
        base = 32 * f + 16 * c
        if part == 0:
            planes[base : base + 8, pl.ds(lanes, value.shape[1])] = value
            planes[base + 8 : base + 16, pl.ds(middle + lanes, value.shape[1])] = value
        else:
            planes[base : base + 8, pl.ds(middle + lanes, value.shape[1])] = -value
            planes[base + 8 : base + 16, pl.ds(lanes, value.shape[1])] = value

    def transform(high, low, result):
        total = None
        for f in range(2):
            value = planes[...]
            mine = lax.broadcasted_iota(jnp.int32, value.shape, 0) // 32 == f
            value = jnp.where(mine, value, 0.0)
            upper = value.astype(jnp.bfloat16)
            lower = (value - upper.astype(jnp.float32)).astype(jnp.bfloat16)
            right = jnp.concatenate([upper, lower], axis=0)
            dims = (((1,), (1,)), ((), ()))
            first = lax.dot_general(high[f], right, dims, preferred_element_type=jnp.float32)
            second = lax.dot_general(low[f], right, dims, preferred_element_type=jnp.float32)
            part = first + pltpu.roll(first, 64, 1) + second
            total = part if total is None else total + part
        result[...] = total

    def tile(ref, index):
        return ref.at[pl.ds(pl.multiple_of(8 * index, 8), 8), :]

    @pl.when(at_exit)
    def _():
        for item in tables:
            item.wait()
        accumulate(STEPS)
        for index in range(8):
            place_plane(index, spec[index], 0)
        transform(col_high, col_low, out_a)

        def send_a(peer, may_be_own):
            item = pltpu.make_async_remote_copy(
                src_ref=tile(out_a, peer), dst_ref=in_a.at[pos_x], send_sem=tail_send.at[0],
                recv_sem=tail_recv.at[0], device_id=(exit_z, peer), device_id_type=MESH,
            )
            begin(peer != pos_x, item) if may_be_own else item.start()

        for_peers(send_a)
        in_a[pos_x] = out_a[pl.ds(pl.multiple_of(8 * pos_x, 8), 8), :]
        others = in_a.at[pl.ds(0, count_x - 1)]
        whole = pltpu.make_async_remote_copy(
            src_ref=others, dst_ref=others, send_sem=tail_send.at[0], recv_sem=tail_recv.at[0],
            device_id=(exit_z, pos_x), device_id_type=MESH,
        )
        whole.wait_recv()
        whole.wait_send()
        for block in range(count_x // 16):
            values = [in_a[16 * block + j] for j in range(16)]
            for index in range(8):
                lined = jnp.zeros((8, 128), jnp.float32)
                for j in range(16):
                    moved = pltpu.roll(values[j], (8 * (j - index)) % 128, 1) if j != index else values[j]
                    lined = jnp.where(lane_group == j, moved, lined)
                place_plane(index, lined, 128 * block)
        transform(row_high, row_low, out_b)
        mine = lax.rem(pos_x, group)

        def send_b(peer, may_be_own):
            item = pltpu.make_async_remote_copy(
                src_ref=tile(out_b, peer), dst_ref=in_b.at[mine], send_sem=tail_send.at[1],
                recv_sem=tail_recv.at[1], device_id=(target_z, peer), device_id_type=MESH,
            )
            begin((target_z != exit_z) | (peer != pos_x), item) if may_be_own else item.start()

        for_peers(send_b)

        @pl.when(target_z == exit_z)
        def _():
            in_b[mine] = out_b[pl.ds(pl.multiple_of(8 * pos_x, 8), 8), :]

    def arrived(number):
        return pltpu.make_async_remote_copy(
            src_ref=in_a.at[pl.ds(0, number)], dst_ref=in_b.at[pl.ds(0, number)], send_sem=tail_send.at[1],
            recv_sem=tail_recv.at[1], device_id=(exit_z, pos_x), device_id_type=MESH,
        )

    own = at_exit & (target_z == exit_z)

    @pl.when(own)
    def _():
        arrived(group - 1).wait_recv()

    @pl.when(jnp.logical_not(own))
    def _():
        arrived(group).wait_recv()

    columns = image.shape[2]
    values = [in_b[j] for j in range(group)]
    for index in range(8):
        lined = jnp.zeros((8, 128), jnp.float32)
        for j in range(group):
            moved = pltpu.roll(values[j], (8 * (j - index)) % 128, 1) if j != index else values[j]
            lined = jnp.where(lane_group == j, moved, lined)
        image[:, index, :] = lined[:wide, :columns]

    def sent(number):
        return pltpu.make_async_remote_copy(
            src_ref=in_a.at[pl.ds(0, number)], dst_ref=in_a.at[pl.ds(0, number)], send_sem=tail_send.at[1],
            recv_sem=tail_recv.at[1], device_id=(exit_z, pos_x), device_id_type=MESH,
        )

    leave.wait()

    @pl.when(own)
    def _():
        sent(count_x - 1).wait_send()

    @pl.when(at_exit & jnp.logical_not(own))
    def _():
        sent(count_x).wait_send()


def march(count_z, count_x, fields, material, mask, eps_table, kerr_table):
    _, wide, deep, span = fields.shape
    vmem = pl.BlockSpec(memory_space=pltpu.VMEM)
    f32 = jnp.float32
    tables = chirp(span, span) + chirp(count_x * wide, wide)
    return pl.pallas_call(
        functools.partial(step_kernel, count_z, count_x),
        out_shape=(
            jax.ShapeDtypeStruct(fields.shape, f32),
            jax.ShapeDtypeStruct((wide, 8, span // count_z), f32),
        ),
        in_specs=[pl.BlockSpec(memory_space=pl.ANY)] * 9,
        out_specs=(pl.BlockSpec(memory_space=pl.ANY), vmem),
        scratch_shapes=[
            pltpu.VMEM(fields.shape, f32),
            pltpu.VMEM((8, 8, span), f32),
            *(pltpu.VMEM(table.shape, jnp.bfloat16) for table in tables),
            pltpu.SemaphoreType.DMA((4,)),
            pltpu.VMEM((64, 2 * max(span, 8 * count_x)), f32),
            pltpu.VMEM((span, 128), f32),
            pltpu.VMEM((count_x, 8, 128), f32),
            pltpu.VMEM((8 * count_x, 128), f32),
            pltpu.VMEM((count_x // count_z, 8, 128), f32),
            pltpu.SemaphoreType.DMA((2,)),
            pltpu.SemaphoreType.DMA((2,)),
            pltpu.VMEM((wide, deep, span), jnp.int32),
            pltpu.VMEM((wide, deep, span), jnp.int32),
            pltpu.SMEM(eps_table.shape, f32),
            pltpu.SMEM(kerr_table.shape, f32),
            pltpu.SMEM((STEPS,), f32),
            pltpu.SMEM((4 * STEPS + 4,), f32),
            pltpu.SemaphoreType.DMA((5,)),
            pltpu.VMEM((wide, deep, span), f32),
            pltpu.VMEM((wide, deep, span), f32),
            pltpu.VMEM((wide, deep, span), f32),
            pltpu.VMEM((wide, deep, span), f32),
            pltpu.VMEM((2, 8, span), f32),
            pltpu.VMEM((2, 8, span), f32),
            pltpu.VMEM((2, 8, span), f32),
            pltpu.VMEM((2, 2, 2, span), f32),
            pltpu.VMEM((2, span), f32),
            pltpu.VMEM((2, 9, 8, span), f32),
            pltpu.VMEM((4, 2, 2, span), f32),
            pltpu.SemaphoreType.DMA((7,)),
            pltpu.SemaphoreType.DMA((2, 7)),
            pltpu.SemaphoreType.DMA((2, 2)),
            pltpu.SemaphoreType.DMA((4, 2)),
        ],
        compiler_params=pltpu.CompilerParams(
            collective_id=1, has_side_effects=True, vmem_limit_bytes=60 * 1024 * 1024
        ),
        name="march",
    )(fields, material, mask, eps_table, kerr_table, *(jnp.asarray(table) for table in tables))


def local(fields, material, source_mask, eps_table, kerr_table):
    count_x, count_z = lax.axis_size("lat"), lax.axis_size("depth")
    return march(count_z, count_x, fields, material, source_mask, eps_table, kerr_table)


def solution(mesh):
    placed = (P(None, "lat", "depth", None), P("lat", "depth", None), P("lat", "depth", None), P(), P())
    return jax.shard_map(
        local, mesh=mesh, in_specs=placed,
        out_specs=(P(None, "lat", "depth", None), P("lat", None, "depth")), check_vma=False,
    )
```

```python
import functools
import math

import jax
import jax.numpy as jnp
import numpy as np
from jax import lax
from jax.experimental import pallas as pl
from jax.experimental.pallas import tpu as pltpu
from jax.sharding import PartitionSpec as P

STEPS = 16
COURANT = 0.55
OMEGAS = (0.9, 1.3)
QUARTERS = (3, 5)
MESH = pl.DeviceIdType.MESH


def pulses():
    middle = np.arange(STEPS) + 0.5
    return np.asarray(np.sin(OMEGAS[0] * middle) + np.sin(OMEGAS[1] * middle), np.float32)


def turns():
    later = np.arange(STEPS) + 1.0
    parts = []
    for omega in OMEGAS:
        parts += [np.cos(omega * later), -np.sin(omega * later)]
    return np.asarray(np.stack(parts, axis=1), np.float32)


def split(table):
    high = table.astype(jnp.bfloat16)
    return high, (table - high.astype(np.float32)).astype(jnp.bfloat16)


def chirp(length, run):
    gap = np.arange(length)[:, None] - np.arange(length)[None, :]
    padded = -(-run // 8) * 8
    tables = []
    for quarter in QUARTERS:
        phase = (quarter * gap * gap % (8 * length)) * (math.pi / (4.0 * length))
        table = np.stack([np.cos(phase), np.sin(phase)], axis=1) / math.sqrt(length)
        table = table.reshape(length // run, run, 2, length // run, run)
        table = np.pad(table, ((0, 0), (0, padded - run), (0, 0), (0, 0), (0, padded - run)))
        tables.append(table.reshape(length // run * padded, 2 * (length // run) * padded))
    return split(np.asarray(np.stack(tables), np.float32))


def step_kernel(
    count_z, count_x,
    fields_hbm, material_hbm, mask_hbm, eps_hbm, kerr_hbm, col_high_hbm, col_low_hbm, row_high_hbm, row_low_hbm,
    fields_out, image,
    state, spec, col_high, col_low, row_high, row_low, table_sem, planes, out_a, in_a, out_b, in_b, tail_send, tail_recv,
    material_ref, mask_ref, eps_ref, kerr_ref, pulse_ref, turn_ref, load_sem,
    eps_v, kerr_v, src_v, fac_v,
    rows_e, rows_h, rows_top, corner_s, mix,
    in_all, in_c, send_sem, recv_sem, corner_send, corner_recv,
):
    wide = state.shape[1]
    span = state.shape[3]
    last = wide - 1
    pos_z = lax.axis_index("depth")
    pos_x = lax.axis_index("lat")
    has_lx, has_hx = pos_x > 0, pos_x < count_x - 1
    has_lz, has_hz = pos_z > 0, pos_z < count_z - 1
    has_a, has_b = has_lz & has_hx, has_hz & has_lx
    low_x, high_x, low_z, high_z = pos_x - 1, pos_x + 1, pos_z - 1, pos_z + 1
    to_lx, to_hx = (pos_z, low_x), (pos_z, high_x)
    to_lz, to_hz = (low_z, pos_x), (high_z, pos_x)
    to_a, to_b = (low_z, high_x), (high_z, low_x)
    neighbours = (
        (has_lx, to_lx), (has_hx, to_hx), (has_lz, to_lz), (has_hz, to_hz), (has_a, to_a), (has_b, to_b)
    )

    loads = [
        pltpu.make_async_copy(source, there, load_sem.at[i])
        for i, (source, there) in enumerate((
            (material_hbm, material_ref), (mask_hbm, mask_ref), (eps_hbm, eps_ref), (kerr_hbm, kerr_ref),
            (fields_hbm, state),
        ))
    ]
    for item in loads:
        item.start()
    mix[...] = jnp.zeros_like(mix)
    in_all[...] = jnp.zeros_like(in_all)
    in_c[...] = jnp.zeros_like(in_c)

    def begin(has, item):
        @pl.when(has)
        def _():
            item.start()

    def for_peers(act):
        side = 4 if count_x == 64 else 2
        runs = count_x // (side * side)
        x, z, y = pos_x // (side * runs), pos_x // side % runs, pos_x % side
        order = (2, 1, 3, 0) if side == 4 else (1, 0)
        at_x = [lax.rem(x + far, side) * (side * runs) for far in order]
        at_y = [lax.rem(y + far, side) for far in order]

        def run(k, carry):
            at_z = jnp.where(z < runs // 2, runs - 1 - k, k) * side
            for i in range(side):
                for j in range(side):
                    act(at_x[i] + at_z + at_y[j], i == side - 1 and j == side - 1)
            return carry

        lax.fori_loop(0, runs, run, 0)

    barrier = pltpu.get_barrier_semaphore()
    exit_z = count_z - 1
    at_exit = pos_z == exit_z
    group = count_x // count_z
    for j in range(group):
        sender = pos_z * group + j
        @pl.when(jnp.logical_not(at_exit & (sender == pos_x)))
        def _():
            pl.semaphore_signal(barrier, inc=1, device_id=(exit_z, sender), device_id_type=MESH)

    tables = [
        pltpu.make_async_copy(source, there, table_sem.at[i])
        for i, (source, there) in enumerate((
            (col_high_hbm, col_high), (col_low_hbm, col_low), (row_high_hbm, row_high), (row_low_hbm, row_low)
        ))
    ]

    @pl.when(at_exit)
    def _():
        def greet(peer, may_be_own):
            def signal():
                pl.semaphore_signal(barrier, inc=1, device_id=(exit_z, peer), device_id_type=MESH)

            pl.when(peer != pos_x)(signal) if may_be_own else signal()

        for_peers(greet)

    for has, target in neighbours:
        @pl.when(has)
        def _():
            pl.semaphore_signal(barrier, inc=1, device_id=target, device_id_type=MESH)

    @pl.when(at_exit)
    def _():
        for item in tables:
            item.start()

    for n in range(STEPS):
        pulse_ref[n] = jnp.float32(pulses()[n])
        for i in range(4):
            turn_ref[4 * n + 4 + i] = jnp.float32(turns()[n, i])
    for i in range(4):
        turn_ref[i] = jnp.float32(0.0)
    for item in loads:
        item.wait()
    material = material_ref[...]
    eps, kerr = jnp.zeros(material.shape, jnp.float32), jnp.zeros(material.shape, jnp.float32)
    for level in range(eps_ref.shape[0]):
        eps = jnp.where(material == level, eps_ref[level], eps)
        kerr = jnp.where(material == level, kerr_ref[level], kerr)
    eps_v[...] = eps
    kerr_v[...] = kerr
    src_v[...] = mask_ref[...].astype(jnp.float32)
    spec[...] = jnp.zeros_like(spec)
    rows_top[...] = jnp.zeros_like(rows_top)

    target_z = pos_x // group
    greeted = sum(jnp.where(has, 1, 0) for has, _ in neighbours)
    greeted += jnp.where(at_exit, 2 * count_x - 1 - jnp.where(target_z == exit_z, 1, 0), 0)
    pl.semaphore_wait(barrier, greeted)

    row = lax.broadcasted_iota(jnp.int32, (8, span), 0)
    col = lax.broadcasted_iota(jnp.int32, (8, span), 1)
    top_row, first_row = row == 7, row == 0
    top_col, first_col = col == span - 1, col == 0
    s = jnp.float32(COURANT)
    keep_lx = jnp.where(has_lx, 1.0, 0.0).astype(jnp.float32)
    keep_lz = jnp.where(has_lz, 1.0, 0.0).astype(jnp.float32)
    keep_hx = jnp.where(has_hx, 1.0, 0.0).astype(jnp.float32)
    keep_hz = jnp.where(has_hz, 1.0, 0.0).astype(jnp.float32)

    def next_y(f):
        return jnp.where(top_col, 0.0, pltpu.roll(f, span - 1, 1))

    def prev_y(f):
        return jnp.where(first_col, 0.0, pltpu.roll(f, 1, 1))

    def next_z(f):
        return jnp.where(top_row, 0.0, pltpu.roll(f, 7, 0))

    def wide_row(r):
        return jnp.broadcast_to(r, (8, span))

    def prev_row(r):
        return jnp.where(first_col[0:1], 0.0, pltpu.roll(r, 1, 1))

    def corner(when, place):
        return pltpu.make_async_remote_copy(
            src_ref=corner_s.at[lax.rem(when, 2), place], dst_ref=in_c.at[lax.rem(when, 4), place],
            send_sem=corner_send.at[lax.rem(when, 2), place], recv_sem=corner_recv.at[lax.rem(when, 4), place],
            device_id=(to_a, to_b)[place], device_id_type=MESH,
        )

    corner_s[...] = jnp.zeros_like(corner_s)
    corner_s[0, 0, 0:1, :] = state[0, last, 0:1, :]
    corner_s[0, 1, 0:1, :] = state[2, 0, 7:8, :]
    begin(has_a, corner(0, 0))
    begin(has_b, corner(0, 1))

    half = wide // 2

    def keep_rows(x, ex, ey, ez):
        part, place = x // half, x % half
        rows_e[part, place : place + 1, :] = ex[0:1, :]
        rows_e[part, half + place : half + place + 1, :] = ey[0:1, :]
        if x == 0:
            rows_e[0, 2 * half : 2 * half + 1, :] = ez[0:1, :]

    def advance_h(x):
        ex, ey, ez = state[0, x], state[1, x], state[2, x]
        if x < last:
            ahead_y, ahead_z = state[1, x + 1], state[2, x + 1]
        else:
            ahead_y, ahead_z = jnp.zeros_like(ey), jnp.zeros_like(ez)
        hx = state[3, x] - s * ((next_y(ez) - ez) - (next_z(ey) - ey))
        hy = state[4, x] - s * ((next_z(ex) - ex) - (ahead_z - ez))
        hz = state[5, x] - s * ((ahead_y - ey) - (next_y(ex) - ex))
        state[3, x] = hx
        state[4, x] = hy
        state[5, x] = hz
        part, place = x // half, x % half
        rows_h[part, place : place + 1, :] = hx[7:8, :]
        rows_h[part, half + place : half + place + 1, :] = hy[7:8, :]

    def copies(n):
        slot = lax.rem(n, 2)

        def copy(index, source, target, there):
            return pltpu.make_async_remote_copy(
                src_ref=source, dst_ref=there, send_sem=send_sem.at[index], recv_sem=recv_sem.at[slot, index],
                device_id=target, device_id_type=MESH,
            )

        first, second = slice(0, 2 * half + 1), slice(0, 2 * half)
        return {
            "xe": (copy(0, state.at[1:3, 0], to_lx, in_all.at[slot, 0:2]), has_lx, has_hx),
            "xr": (copy(1, rows_e.at[0, 0:1], to_lx, in_all.at[slot, 8, 0:1]), has_lx, has_hx),
            "xh": (copy(2, state.at[4:6, last], to_hx, in_all.at[slot, 2:4]), has_hx, has_lx),
            "ze0": (copy(3, rows_e.at[0, first], to_lz, in_all.at[slot, 4, first]), has_lz, has_hz),
            "ze1": (copy(4, rows_e.at[1, second], to_lz, in_all.at[slot, 5, second]), has_lz, has_hz),
            "zh0": (copy(5, rows_h.at[0, second], to_hz, in_all.at[slot, 6, second]), has_hz, has_lz),
            "zh1": (copy(6, rows_h.at[1, second], to_hz, in_all.at[slot, 7, second]), has_hz, has_lz),
        }

    def send(items, *names):
        for name in names:
            item, has_to, _ = items[name]
            begin(has_to, item)

    def receive(items, *names):
        for name in names:
            item, _, has_from = items[name]
            pl.when(has_from)(item.wait_recv)

    def accumulate(n):
        for x in range(wide):
            rows_top[0, x : x + 1, :] = state[0, x, 7:8, :]
            rows_top[1, x : x + 1, :] = state[1, x, 7:8, :]
        for f in range(2):
            for part in range(2):
                weight = turn_ref[4 * n + 2 * f + part]
                for c in range(2):
                    spec[4 * f + 2 * c + part] += weight * rows_top[c]

    for x in range(wide):
        keep_rows(x, state[0, x], state[1, x], state[2, x])
    started = copies(0)
    send(started, "ze0", "ze1", "xe", "xr")
    for x in range(wide):
        advance_h(x)
    send(started, "zh0", "zh1", "xh")

    def one_step(n, more):
        slot = lax.rem(n, 2)
        now, later = copies(n), copies(n + 1) if more else {}

        @pl.when(at_exit)
        def _():
            accumulate(n)

        for x in range(wide):
            ex, ey, ez = state[0, x], state[1, x], state[2, x]
            fac_v[x] = s / (eps_v[x] + kerr_v[x] * (ex * ex + ey * ey + ez * ez))

        pulse = pulse_ref[n]
        ahead = n + 1
        side = lax.rem(ahead, 2)
        if more:
            corner_s[side, 0, 0:1, :] = (
                state[0, last, 0:1, :] + src_v[last, 0:1, :] * pulse + fac_v[last, 0:1, :]
                * (state[5, last, 0:1, :] - prev_row(state[5, last, 0:1, :]) - state[4, last, 0:1, :])
            )
            corner_s[side, 0, 1:2, :] = fac_v[last, 0:1, :]
            corner_s[side, 1, 0:1, :] = state[2, 0, 7:8, :] + fac_v[0, 7:8, :] * (
                state[4, 0, 7:8, :] - (state[3, 0, 7:8, :] - prev_row(state[3, 0, 7:8, :]))
            )
            corner_s[side, 1, 1:2, :] = fac_v[0, 7:8, :]
            begin(has_a, corner(ahead, 0))
            begin(has_b, corner(ahead, 1))

        for item, has_to, _ in now.values():
            pl.when(has_to)(item.wait_send)
        def complete_z(x):
            part, place = x // half, x % half
            above_x = wide_row(in_all[slot, 4 + part, place : place + 1, :])
            above_y = wide_row(in_all[slot, 4 + part, half + place : half + place + 1, :])
            hx = state[3, x] + jnp.where(top_row, (s * keep_hz) * above_y, 0.0)
            hy = state[4, x] - jnp.where(top_row, (s * keep_hz) * above_x, 0.0)
            return hx, hy, state[5, x]

        def advance_e(x, magnetic, before_y, before_z, corner_row):
            part, place = x // half, x % half
            hx, hy, hz = magnetic
            ex, ey, ez = state[0, x], state[1, x], state[2, x]
            below_x = wide_row(in_all[slot, 6 + part, place : place + 1, :]) + s * ey
            below_y = wide_row(in_all[slot, 6 + part, half + place : half + place + 1, :]) - s * ex
            if x == last:
                hy = hy + (s * keep_hx) * in_all[slot, 1]
                hz = hz - (s * keep_hx) * in_all[slot, 0]
                below_y = below_y + s * wide_row(keep_hx * corner_row)
                face = in_all[slot, 0, 0:1, :]
                mix[1:2, :] = -below_y[0:1, :] - s * in_all[slot, 8, 0:1, :] - s * (face - prev_row(face))
            down_x = jnp.where(first_row, keep_lz * below_x, pltpu.roll(hx, 1, 0))
            down_y = jnp.where(first_row, keep_lz * below_y, pltpu.roll(hy, 1, 0))
            fac = fac_v[x]
            ex = ex + fac * ((hz - prev_y(hz)) - (hy - down_y)) + src_v[x] * pulse
            ey = ey + fac * ((hx - down_x) - (hz - before_z))
            ez = ez + fac * ((hy - before_y) - (hx - prev_y(hx)))
            keep_rows(x, ex, ey, ez)
            state[0, x] = ex
            state[1, x] = ey
            state[2, x] = ez
            state[3, x] = hx
            state[4, x] = hy
            state[5, x] = hz

        receive(now, "ze0", "zh0")
        first_h = complete_z(0)
        before = first_h
        for x in range(1, last):
            if x == half:
                receive(now, "ze1", "zh1")
            magnetic = complete_z(x)
            advance_e(x, magnetic, before[1], before[2], None)
            before = magnetic
            if more and x > 1:
                advance_h(x - 1)

        for place, has_to, has_from in ((0, has_a, has_b), (1, has_b, has_a)):
            pl.when(has_to)(corner(n, place).wait_send)
            pl.when(has_from)(corner(n, place).wait_recv)
        here = lax.rem(n, 4)
        corner_ex = in_c[here, 0, 0:1, :] + in_c[here, 0, 1:2, :] * mix[0:1, :]
        corner_ez = in_c[here, 1, 0:1, :] + in_c[here, 1, 1:2, :] * mix[1:2, :]
        receive(now, "xe", "xr")
        advance_e(last, complete_z(last), before[1], before[2], corner_ez)
        if more:
            advance_h(last)
            send(later, "xh")
        receive(now, "xh")
        ex, ey, ez = state[0, 0], state[1, 0], state[2, 0]
        corner_x = jnp.where(top_row, wide_row(keep_hz * corner_ex), 0.0)
        before_y = keep_lx * (in_all[slot, 2] + s * ez - s * corner_x)
        before_z = keep_lx * (in_all[slot, 3] - s * ey)
        face = in_all[slot, 4, half : half + 1, :]
        mix[0:1, :] = (
            before_y[7:8, :] - s * (face - prev_row(face)) - s * in_all[slot, 4, 2 * half : 2 * half + 1, :]
        )
        advance_e(0, first_h, before_y, before_z, None)
        if more:
            send(later, "xe", "xr", "ze0")
        if more:
            send(later, "ze1")
            advance_h(0)
            send(later, "zh0")
            advance_h(last - 1)
            send(later, "zh1")

    def full_step(n, carry):
        one_step(n, True)
        return carry

    lax.fori_loop(0, STEPS - 1, full_step, 0)
    one_step(STEPS - 1, False)
    leave = pltpu.make_async_copy(state, fields_out, load_sem.at[0])
    leave.start()

    lane_group = lax.broadcasted_iota(jnp.int32, (8, 128), 1) // 8
    middle = planes.shape[1] // 2

    def place_plane(index, value, lanes):
        f, c, part = index // 4, index // 2 % 2, index % 2
        base = 32 * f + 16 * c
        if part == 0:
            planes[base : base + 8, pl.ds(lanes, value.shape[1])] = value
            planes[base + 8 : base + 16, pl.ds(middle + lanes, value.shape[1])] = value
        else:
            planes[base : base + 8, pl.ds(middle + lanes, value.shape[1])] = -value
            planes[base + 8 : base + 16, pl.ds(lanes, value.shape[1])] = value

    def transform(high, low, result):
        total = None
        for f in range(2):
            value = planes[...]
            mine = lax.broadcasted_iota(jnp.int32, value.shape, 0) // 32 == f
            value = jnp.where(mine, value, 0.0)
            upper = value.astype(jnp.bfloat16)
            lower = (value - upper.astype(jnp.float32)).astype(jnp.bfloat16)
            right = jnp.concatenate([upper, lower], axis=0)
            dims = (((1,), (1,)), ((), ()))
            first = lax.dot_general(high[f], right, dims, preferred_element_type=jnp.float32)
            second = lax.dot_general(low[f], right, dims, preferred_element_type=jnp.float32)
            part = first + pltpu.roll(first, 64, 1) + second
            total = part if total is None else total + part
        result[...] = total

    def tile(ref, index):
        return ref.at[pl.ds(pl.multiple_of(8 * index, 8), 8), :]

    @pl.when(at_exit)
    def _():
        for item in tables:
            item.wait()
        accumulate(STEPS)
        for index in range(8):
            place_plane(index, spec[index], 0)
        transform(col_high, col_low, out_a)

        def send_a(peer, may_be_own):
            item = pltpu.make_async_remote_copy(
                src_ref=tile(out_a, peer), dst_ref=in_a.at[pos_x], send_sem=tail_send.at[0],
                recv_sem=tail_recv.at[0], device_id=(exit_z, peer), device_id_type=MESH,
            )
            begin(peer != pos_x, item) if may_be_own else item.start()

        for_peers(send_a)
        in_a[pos_x] = out_a[pl.ds(pl.multiple_of(8 * pos_x, 8), 8), :]
        others = in_a.at[pl.ds(0, count_x - 1)]
        whole = pltpu.make_async_remote_copy(
            src_ref=others, dst_ref=others, send_sem=tail_send.at[0], recv_sem=tail_recv.at[0],
            device_id=(exit_z, pos_x), device_id_type=MESH,
        )
        whole.wait_recv()
        whole.wait_send()
        for block in range(count_x // 16):
            values = [in_a[16 * block + j] for j in range(16)]
            for index in range(8):
                lined = jnp.zeros((8, 128), jnp.float32)
                for j in range(16):
                    moved = pltpu.roll(values[j], (8 * (j - index)) % 128, 1) if j != index else values[j]
                    lined = jnp.where(lane_group == j, moved, lined)
                place_plane(index, lined, 128 * block)
        transform(row_high, row_low, out_b)
        mine = lax.rem(pos_x, group)

        def send_b(peer, may_be_own):
            item = pltpu.make_async_remote_copy(
                src_ref=tile(out_b, peer), dst_ref=in_b.at[mine], send_sem=tail_send.at[1],
                recv_sem=tail_recv.at[1], device_id=(target_z, peer), device_id_type=MESH,
            )
            begin((target_z != exit_z) | (peer != pos_x), item) if may_be_own else item.start()

        for_peers(send_b)

        @pl.when(target_z == exit_z)
        def _():
            in_b[mine] = out_b[pl.ds(pl.multiple_of(8 * pos_x, 8), 8), :]

    def arrived(number):
        return pltpu.make_async_remote_copy(
            src_ref=in_a.at[pl.ds(0, number)], dst_ref=in_b.at[pl.ds(0, number)], send_sem=tail_send.at[1],
            recv_sem=tail_recv.at[1], device_id=(exit_z, pos_x), device_id_type=MESH,
        )

    own = at_exit & (target_z == exit_z)

    @pl.when(own)
    def _():
        arrived(group - 1).wait_recv()

    @pl.when(jnp.logical_not(own))
    def _():
        arrived(group).wait_recv()

    columns = image.shape[2]
    values = [in_b[j] for j in range(group)]
    for index in range(8):
        lined = jnp.zeros((8, 128), jnp.float32)
        for j in range(group):
            moved = pltpu.roll(values[j], (8 * (j - index)) % 128, 1) if j != index else values[j]
            lined = jnp.where(lane_group == j, moved, lined)
        image[:, index, :] = lined[:wide, :columns]

    def sent(number):
        return pltpu.make_async_remote_copy(
            src_ref=in_a.at[pl.ds(0, number)], dst_ref=in_a.at[pl.ds(0, number)], send_sem=tail_send.at[1],
            recv_sem=tail_recv.at[1], device_id=(exit_z, pos_x), device_id_type=MESH,
        )

    leave.wait()

    @pl.when(own)
    def _():
        sent(count_x - 1).wait_send()

    @pl.when(at_exit & jnp.logical_not(own))
    def _():
        sent(count_x).wait_send()


def march(count_z, count_x, fields, material, mask, eps_table, kerr_table):
    _, wide, deep, span = fields.shape
    vmem = pl.BlockSpec(memory_space=pltpu.VMEM)
    f32 = jnp.float32
    tables = chirp(span, span) + chirp(count_x * wide, wide)
    return pl.pallas_call(
        functools.partial(step_kernel, count_z, count_x),
        out_shape=(
            jax.ShapeDtypeStruct(fields.shape, f32),
            jax.ShapeDtypeStruct((wide, 8, span // count_z), f32),
        ),
        in_specs=[pl.BlockSpec(memory_space=pl.ANY)] * 9,
        out_specs=(pl.BlockSpec(memory_space=pl.ANY), vmem),
        scratch_shapes=[
            pltpu.VMEM(fields.shape, f32),
            pltpu.VMEM((8, 8, span), f32),
            *(pltpu.VMEM(table.shape, jnp.bfloat16) for table in tables),
            pltpu.SemaphoreType.DMA((4,)),
            pltpu.VMEM((64, 2 * max(span, 8 * count_x)), f32),
            pltpu.VMEM((span, 128), f32),
            pltpu.VMEM((count_x, 8, 128), f32),
            pltpu.VMEM((8 * count_x, 128), f32),
            pltpu.VMEM((count_x // count_z, 8, 128), f32),
            pltpu.SemaphoreType.DMA((2,)),
            pltpu.SemaphoreType.DMA((2,)),
            pltpu.VMEM((wide, deep, span), jnp.int32),
            pltpu.VMEM((wide, deep, span), jnp.int32),
            pltpu.SMEM(eps_table.shape, f32),
            pltpu.SMEM(kerr_table.shape, f32),
            pltpu.SMEM((STEPS,), f32),
            pltpu.SMEM((4 * STEPS + 4,), f32),
            pltpu.SemaphoreType.DMA((5,)),
            pltpu.VMEM((wide, deep, span), f32),
            pltpu.VMEM((wide, deep, span), f32),
            pltpu.VMEM((wide, deep, span), f32),
            pltpu.VMEM((wide, deep, span), f32),
            pltpu.VMEM((2, 8, span), f32),
            pltpu.VMEM((2, 8, span), f32),
            pltpu.VMEM((2, 8, span), f32),
            pltpu.VMEM((2, 2, 2, span), f32),
            pltpu.VMEM((2, span), f32),
            pltpu.VMEM((2, 9, 8, span), f32),
            pltpu.VMEM((4, 2, 2, span), f32),
            pltpu.SemaphoreType.DMA((7,)),
            pltpu.SemaphoreType.DMA((2, 7)),
            pltpu.SemaphoreType.DMA((2, 2)),
            pltpu.SemaphoreType.DMA((4, 2)),
        ],
        compiler_params=pltpu.CompilerParams(
            collective_id=1, has_side_effects=True, vmem_limit_bytes=60 * 1024 * 1024
        ),
        name="march",
    )(fields, material, mask, eps_table, kerr_table, *(jnp.asarray(table) for table in tables))


def hand_over_kernel(fields_ref, image_ref, fields_out, image_out, fields_v, image_v, into, out):
    stages = [
        (
            pltpu.make_async_copy(fields_ref.at[i], fields_v.at[i], into.at[i]),
            pltpu.make_async_copy(fields_v.at[i], fields_out.at[i], out.at[i]),
        )
        for i in range(6)
    ]
    stages.append((
        pltpu.make_async_copy(image_ref, image_v, into.at[6]), pltpu.make_async_copy(image_v, image_out, out.at[6])
    ))
    for first, _ in stages:
        first.start()
    for first, second in stages:
        first.wait()
        second.start()
    for _, second in stages:
        second.wait()


def hand_over(fields, image):
    anywhere = pl.BlockSpec(memory_space=pl.ANY)
    return pl.pallas_call(
        hand_over_kernel,
        out_shape=(
            jax.ShapeDtypeStruct(fields.shape, jnp.float32), jax.ShapeDtypeStruct(image.shape, jnp.float32)
        ),
        in_specs=[anywhere] * 2,
        out_specs=(anywhere,) * 2,
        scratch_shapes=[
            pltpu.VMEM(fields.shape, jnp.float32),
            pltpu.VMEM(image.shape, jnp.float32),
            pltpu.SemaphoreType.DMA((7,)),
            pltpu.SemaphoreType.DMA((7,)),
        ],
        compiler_params=pltpu.CompilerParams(vmem_limit_bytes=60 * 1024 * 1024),
        name="hand_over",
    )(fields, image)


def local(fields, material, source_mask, eps_table, kerr_table):
    count_x, count_z = lax.axis_size("lat"), lax.axis_size("depth")
    return hand_over(*march(count_z, count_x, fields, material, source_mask, eps_table, kerr_table))


def solution(mesh):
    placed = (P(None, "lat", "depth", None), P("lat", "depth", None), P("lat", "depth", None), P(), P())
    return jax.shard_map(
        local, mesh=mesh, in_specs=placed,
        out_specs=(P(None, "lat", "depth", None), P("lat", None, "depth")), check_vma=False,
    )
```
